128 devices in a mesh: grp: 4 (over x), dev: 32 (over y, z, core).
Axes of the slice: x: 4, y: 4, z: 4, core: 2. Of those that a mesh axis runs over, the one named last changes fastest.
Arguments:
- tile_list: int32 [256, 3], replicated, may hold values from 0 to 127, as said below
- holder: int32 [128], replicated, may hold values from 0 to 127, each once
- coordinates: float32 [3, 131072], P(None, ('grp', 'dev')), may hold values from -6 to 6
- dissim: bfloat16 [512, 1024, 1024], P(('grp', 'dev')), may hold values from 0.5 to 4
Outputs:
- guttman: float32 [3, 131072], P(None, ('grp', 'dev'))
- stress: float32 [], replicated
The draws below stay inside these ranges and needn't reach their ends.
Inputs may be any that keep to these rules, and one draw needn't show every extreme that they name: `tile_list`: rows are distinct pairs with row block less than column block; every block is in exactly 4 tiles; each device owns 1, 2 or 4 tiles, a quarter of the devices own 4.
All inputs are finite; a program needn't handle non-finite values.
Results may differ from the reference program's by a relative error of at most 0.0003.
Values sent between devices are 32-bit elements; how exact they have to be, the bound alone decides.
No kernel may reach another device: no remote copies, remote signals or barrier semaphores. Data moves between devices by JAX's collectives and lax.ppermute only.
A program may use at most 192 MiB of HBM per device.

```python
import jax
import jax.numpy as jnp
from jax import lax

DIM = 3
TB = 1024
SLOTS = 4
NB = 128
NPTS = 131072
NTILES = 256


def draw_tile_list(key, part):
    key = jax.random.fold_in(key, 11)
    key_order, key_owner, key_shuffle = jax.random.split(key, 3)
    order = jax.random.permutation(key_order, NB).astype(jnp.int32)
    first = jnp.concatenate([order, order])
    second = jnp.concatenate([jnp.roll(order, -1), jnp.roll(order, -2)])
    row_blocks = jnp.minimum(first, second)
    col_blocks = jnp.maximum(first, second)
    quarter = NB // 4
    counts = jnp.concatenate([jnp.full((quarter,), SLOTS, jnp.int32), jnp.full((2 * quarter,), 1, jnp.int32), jnp.full((NB - 3 * quarter,), 2, jnp.int32)])
    device_order = jax.random.permutation(key_owner, NB).astype(jnp.int32)
    owners = jnp.repeat(device_order, counts, total_repeat_length=NTILES)
    shuffle = jax.random.permutation(key_shuffle, NTILES)
    owners = owners[shuffle]
    return jnp.stack([row_blocks, col_blocks, owners], axis=1).astype(jnp.int32)


def block_scale(stream_key, extent, cuts, smallest, high):
    factor_of, own = 1.0, jax.random.fold_in(stream_key, 6)
    for position, shards_of in cuts:
        steps = jnp.exp(jax.random.uniform(jax.random.fold_in(own, position), (shards_of,), jnp.float32, smallest / len(cuts), high / len(cuts)))
        factor_of = factor_of * jnp.repeat(steps, extent[position] // shards_of).reshape([-1 if axis == position else 1 for axis in range(len(extent))])
    return factor_of


def normal_values(own_key, dims, width, limit, shards=(), kind=jnp.bfloat16):
    drawn = jax.random.normal(own_key, dims, jnp.float32) * width
    if len(shards) > 0:
        drawn = block_scale(own_key, dims, shards, -0.22, 0.18) * drawn
    return jnp.clip(drawn, min=-limit, max=limit).astype(kind)


def setup_inputs(seed: int = 0) -> dict:
    splits = jax.random.split(jax.random.key(seed), 5)
    return {
        "tile_list": draw_tile_list(jax.random.fold_in(splits[4], 71), 0),
        "holder": jax.random.permutation(splits[1], NB).astype(jnp.int32),
        "coordinates": normal_values(splits[2], (DIM, NPTS), 1.0, 6.0, ((1, 128),), jnp.float32),
        "dissim": jnp.clip(0.5 + 3.5 * jax.random.uniform(splits[3], (NB * SLOTS, TB, TB), jnp.float32) ** block_scale(splits[3], (NB * SLOTS, TB, TB), ((0, 128),), -0.2, 0.2), 0.5, 4.0).astype(jnp.bfloat16),
    }


dist_floor = 0.25

def tile_ranks(tile_list):
    owners = tile_list[:, 2]
    indices = jnp.arange(owners.shape[0], dtype=jnp.int32)
    same_owner = owners[:, None] == owners[None, :]
    earlier = indices[None, :] < indices[:, None]
    return lax.optimization_barrier(jnp.sum((same_owner & earlier).astype(jnp.int32), axis=1)).astype(jnp.int32)

def tile_terms(row_coords, col_coords, target):
    squared = jnp.zeros(target.shape, jnp.float32)
    for comp in range(row_coords.shape[0]):
        gap = row_coords[comp][:, None] - col_coords[comp][None, :]
        squared = squared + gap * gap
    distance = jnp.maximum(jnp.sqrt(squared), dist_floor)
    ratio = target / distance
    row_sums = lax.optimization_barrier(jnp.sum(ratio, axis=1))
    col_sums = lax.optimization_barrier(jnp.sum(ratio, axis=0))
    row_cross = lax.dot_general(col_coords, ratio, (((1,), (1,)), ((), ())), precision=lax.Precision.HIGHEST)
    col_cross = lax.dot_general(row_coords, ratio, (((1,), (0,)), ((), ())), precision=lax.Precision.HIGHEST)
    row_part = row_coords * row_sums[None, :] - row_cross
    col_part = col_coords * col_sums[None, :] - col_cross
    error = target - distance
    return (row_part, col_part, jnp.sum(error * error))

def reference(tile_list, holder, coordinates, dissim):
    tile_rank = tile_ranks(tile_list)

    def one_tile(carry, tile_index):
        accumulated, stress_sum = carry
        row_block = tile_list[tile_index, 0]
        col_block = tile_list[tile_index, 1]
        owner = tile_list[tile_index, 2]
        slot = (owner * SLOTS + tile_rank[tile_index]).astype(jnp.int32)
        target = lax.dynamic_index_in_dim(dissim, slot, 0, keepdims=False).astype(jnp.float32)
        row_start = (holder[row_block] * TB).astype(jnp.int32)
        col_start = (holder[col_block] * TB).astype(jnp.int32)
        row_coords = lax.dynamic_slice_in_dim(coordinates, row_start, TB, 1)
        col_coords = lax.dynamic_slice_in_dim(coordinates, col_start, TB, 1)
        row_part, col_part, tile_stress = tile_terms(row_coords, col_coords, target)
        current = lax.dynamic_slice_in_dim(accumulated, row_start, TB, 1)
        accumulated = lax.dynamic_update_slice_in_dim(accumulated, current + row_part, row_start, 1)
        current = lax.dynamic_slice_in_dim(accumulated, col_start, TB, 1)
        accumulated = lax.dynamic_update_slice_in_dim(accumulated, current + col_part, col_start, 1)
        return ((accumulated, stress_sum + tile_stress), None)
    start = (jnp.zeros(coordinates.shape, jnp.float32), jnp.zeros((), jnp.float32))
    (accumulated, stress_sum), _ = lax.scan(one_tile, start, jnp.arange(NTILES, dtype=jnp.int32))
    return (accumulated * (1.0 / TB), stress_sum)
```

```python
import functools

import jax
import jax.numpy as jnp
from jax import lax
from jax.experimental import pallas as pl
from jax.experimental.pallas import tpu as pltpu
from jax.sharding import PartitionSpec as P

AXES = ("grp", "dev")
FLOOR_SQUARED = 0.0625
LANES = 128
DIM = 3
VMEM_LIMIT = 40 * 1024 * 1024


def line_perm(groups, devs, shift):
    return [
        (((g + shift) % groups) * devs + d, g * devs + d)
        for g in range(groups)
        for d in range(devs)
    ]


def core_perm(devices):
    return [(i, i ^ 1) for i in range(devices)]


def plane_groups(groups, devs):
    return [
        [g * devs + 2 * chip + core for chip in range(devs // 2)]
        for g in range(groups)
        for core in range(2)
    ]


def from_line(array, groups, devs):
    own = [array] + [
        lax.ppermute(array, AXES, line_perm(groups, devs, d)) for d in range(1, groups)
    ]
    twin = [lax.ppermute(a, AXES, core_perm(groups * devs)) for a in own]
    return own + twin


def tile_body(rows, width, sc, delta_hbm, *refs):
    sources = refs[:8]
    parts, delta, blocks, wide, row_acc, delta_sem, block_sem = refs[8:]
    slots = delta.shape[0]
    chunks = width // LANES
    half = chunks // 2

    def delta_copy(k):
        return pltpu.make_async_copy(delta_hbm.at[k], delta.at[k], delta_sem.at[k])

    for k in range(slots):
        pl.when(sc[k] > 0)(lambda k=k: delta_copy(k).start())

    def block_copy(s, i, at):
        return pltpu.make_async_copy(sources[s].at[at], blocks.at[i], block_sem.at[i])

    for i in range(2 * slots):
        for s in range(8):
            pl.when(sc[slots + i] == s)(
                lambda i=i, s=s: block_copy(s, i, sc[3 * slots + i]).start()
            )
    for i in range(2 * slots):
        block_copy(0, i, 0).wait()

    parts[2 * slots * DIM * chunks :, :] = jnp.zeros((8, LANES), jnp.float32)

    def one_tile(k, _):
        @pl.when(sc[k] > 0)
        def _():
            delta_copy(k).wait()
            for c in range(DIM):
                for j in range(chunks):
                    row = blocks[2 * k, pl.ds(c * chunks + j, 1), :]
                    wide[c, pl.ds(j * LANES, LANES), :] = jnp.transpose(
                        jnp.broadcast_to(row, (LANES, LANES))
                    )
            stress = jnp.zeros((16, LANES), jnp.float32)
            for h in range(2):
                first = h * half
                cols = [
                    [
                        jnp.broadcast_to(
                            blocks[2 * k + 1, pl.ds(c * chunks + first + j, 1), :],
                            (16, LANES),
                        )
                        for j in range(half)
                    ]
                    for c in range(DIM)
                ]

                def step(p, carry, h=h, first=first, cols=cols):
                    stress, acc = carry
                    at = pl.ds(pl.multiple_of(p * 16, 16), 16)
                    xa = [wide[c, at, :] for c in range(DIM)]
                    acc = [list(a) for a in acc]
                    sums = [None] * DIM
                    for j in range(half):
                        target = delta[
                            k, at, pl.ds((first + j) * LANES, LANES)
                        ].astype(jnp.float32)
                        gaps = [xa[c] - cols[c][j] for c in range(DIM)]
                        squared = gaps[0] * gaps[0]
                        for c in range(1, DIM):
                            squared = squared + gaps[c] * gaps[c]
                        squared = jnp.maximum(squared, FLOOR_SQUARED)
                        inverse = lax.rsqrt(squared)
                        error = target - squared * inverse
                        stress = stress + error * error
                        ratio = target * inverse
                        for c in range(DIM):
                            moved = ratio * gaps[c]
                            acc[c][j] = acc[c][j] + moved
                            sums[c] = moved if sums[c] is None else sums[c] + moved
                    for c in range(DIM):
                        if h == 0:
                            row_acc[c, at, :] = sums[c]
                        else:
                            row_acc[c, at, :] += sums[c]
                    return stress, tuple(tuple(a) for a in acc)

                zero = jnp.zeros((16, LANES), jnp.float32)
                stress, acc = lax.fori_loop(
                    0,
                    rows // 16,
                    step,
                    (stress, tuple(tuple(zero for _ in range(half)) for _ in range(DIM))),
                )
                for c in range(DIM):
                    for j in range(half):
                        parts[pl.ds((2 * k + 1) * DIM * chunks + c * chunks + first + j, 1), :] = (
                            -jnp.sum(acc[c][j], axis=0, keepdims=True)
                        )
            for c in range(DIM):
                for j in range(chunks):
                    turned = jnp.transpose(row_acc[c, pl.ds(j * LANES, LANES), :])
                    parts[pl.ds(2 * k * DIM * chunks + c * chunks + j, 1), :] = jnp.sum(
                        turned, axis=0, keepdims=True
                    )
            parts[2 * slots * DIM * chunks :, :] += stress[:8] + stress[8:]

        return 0

    lax.fori_loop(0, slots, one_tile, 0)


def tile_parts(scalars, dissim, sources):
    slots, rows, width = dissim.shape
    block_rows = DIM * width // LANES
    return pl.pallas_call(
        functools.partial(tile_body, rows, width),
        out_shape=jax.ShapeDtypeStruct((2 * slots * block_rows + 8, LANES), jnp.float32),
        in_specs=[pl.BlockSpec(memory_space=pltpu.SMEM)]
        + [pl.BlockSpec(memory_space=pl.ANY)] * 9,
        out_specs=pl.BlockSpec(memory_space=pltpu.VMEM),
        scratch_shapes=[
            pltpu.VMEM((slots, rows, width), jnp.bfloat16),
            pltpu.VMEM((2 * slots, block_rows, LANES), jnp.float32),
            pltpu.VMEM((DIM, rows, LANES), jnp.float32),
            pltpu.VMEM((DIM, rows, LANES), jnp.float32),
            pltpu.SemaphoreType.DMA((slots,)),
            pltpu.SemaphoreType.DMA((2 * slots,)),
        ],
        compiler_params=pltpu.CompilerParams(vmem_limit_bytes=VMEM_LIMIT),
        name="tile_parts",
    )(scalars, dissim, *sources)


def gather_body(count, block_rows, where, *refs):
    sources, out = refs[:-1], refs[-1]
    stress = sources[0][count * block_rows :, :]
    for s in range(1, len(sources)):
        stress = stress + sources[s][count * block_rows :, :]
    for chip in range(out.shape[0]):
        out[chip, :block_rows, :] = jnp.zeros((block_rows, LANES), jnp.float32)
        out[chip, block_rows:, :] = stress
    for s in range(len(sources)):
        for i in range(count):
            chip = where[s * count + i]

            @pl.when(chip >= 0)
            def _(s=s, i=i, chip=chip):
                out[chip, :block_rows, :] += sources[s][
                    i * block_rows : (i + 1) * block_rows, :
                ]


def by_chip(where, sources, chips):
    rows = sources[0].shape[0] - 8
    count = where.shape[0] // len(sources)
    block_rows = rows // count
    return pl.pallas_call(
        functools.partial(gather_body, count, block_rows),
        out_shape=jax.ShapeDtypeStruct((chips, block_rows + 8, LANES), jnp.float32),
        in_specs=[pl.BlockSpec(memory_space=pltpu.SMEM)]
        + [pl.BlockSpec(memory_space=pltpu.VMEM)] * len(sources),
        out_specs=pl.BlockSpec(memory_space=pltpu.VMEM),
        compiler_params=pltpu.CompilerParams(vmem_limit_bytes=VMEM_LIMIT),
        name="by_chip",
    )(where, *sources)


def total_body(width, pieces, out, stress):
    block_rows = pieces.shape[1] - 8
    chunks = width // LANES
    total = pieces[0]
    for i in range(1, pieces.shape[0]):
        total = total + pieces[i]
    for c in range(DIM):
        for j in range(chunks):
            r = c * chunks + j
            out[c : c + 1, j * LANES : (j + 1) * LANES] = total[r : r + 1, :] * (1.0 / width)
    stress[0, 0] = jnp.sum(total[block_rows:, :])


def total_of(pieces, width):
    return pl.pallas_call(
        functools.partial(total_body, width),
        out_shape=(
            jax.ShapeDtypeStruct((DIM, width), jnp.float32),
            jax.ShapeDtypeStruct((1, 1), jnp.float32),
        ),
        in_specs=[pl.BlockSpec(memory_space=pltpu.VMEM)],
        out_specs=(
            pl.BlockSpec(memory_space=pltpu.VMEM),
            pl.BlockSpec(memory_space=pltpu.SMEM),
        ),
        name="total",
    )(pieces)


def tables(tile_list, holder, groups, devs, slots):
    group, dev = lax.axis_index("grp"), lax.axis_index("dev")
    owners = tile_list[:, 2]
    indices = jnp.arange(owners.shape[0], dtype=jnp.int32)
    earlier = (owners[:, None] == owners[None, :]) & (indices[None, :] < indices[:, None])
    rank = jnp.sum(earlier.astype(jnp.int32), axis=1)
    blocks = jnp.arange(holder.shape[0], dtype=jnp.int32)
    position = jnp.sum(
        jnp.where(tile_list[:, :2, None] == blocks, holder, 0), axis=2
    )
    order = jnp.arange(2 * groups, dtype=jnp.int32)
    line = (group + order) % groups * devs + (dev ^ (order // groups))
    wanted = (line[:, None] * slots + jnp.arange(slots, dtype=jnp.int32)).reshape(-1)
    chosen = wanted[:, None] == (owners * slots + rank)[None, :]
    held = jnp.sum(jnp.where(chosen[:, :, None], position + 1, 0), axis=1).reshape(-1) - 1
    mine = held[: 2 * slots]
    present = (mine[::2] >= 0).astype(jnp.int32)
    at = jnp.maximum(mine, 0)
    source = (at // devs - group) % groups + groups * ((at % 2) ^ (dev % 2))
    for_tiles = jnp.concatenate([present, source, at % devs // 2])
    here = (held >= 0) & (held // devs == group) & (held % 2 == dev % 2)
    where = jnp.where(here, held % devs // 2, -1)
    return for_tiles, where


def on_device(tile_list, holder, coordinates, dissim):
    groups, devs = lax.axis_size("grp"), lax.axis_size("dev")
    chips = devs // 2
    width = coordinates.shape[1]
    slots = dissim.shape[0]
    block_rows = DIM * width // LANES
    plane = plane_groups(groups, devs)
    for_tiles, where = tables(tile_list, holder, groups, devs, slots)
    sent = jnp.broadcast_to(
        coordinates.reshape(1, block_rows, LANES), (chips, block_rows, LANES)
    )
    own = lax.all_to_all(sent, AXES, 0, 0, tiled=True, axis_index_groups=plane)
    parts = tile_parts(for_tiles, dissim, from_line(own, groups, devs))
    pieces = by_chip(where, from_line(parts, groups, devs), chips)
    pieces = lax.all_to_all(pieces, AXES, 0, 0, tiled=True, axis_index_groups=plane)
    guttman, stress = total_of(pieces, width)
    return guttman, stress[0, 0]


def solution(mesh):
    placed = (P(), P(), P(None, AXES), P(AXES, None, None))
    return jax.shard_map(
        on_device,
        mesh=mesh,
        in_specs=placed,
        out_specs=(P(None, AXES), P()),
        check_vma=False,
    )
```

```python
import functools

import jax
import jax.numpy as jnp
from jax import lax
from jax.experimental import pallas as pl
from jax.experimental.pallas import tpu as pltpu
from jax.sharding import PartitionSpec as P

AXES = ("grp", "dev")
FLOOR_SQUARED = 0.0625
LANES = 128
DIM = 3
VMEM_LIMIT = 32 * 1024 * 1024
KDIM = 128
STEP = 128
FETCH = 1024
DEPTH = 512
AHEAD = 1
LAG = 1


def line_perm(groups, devs, shift):
    return [
        (((g + shift) % groups) * devs + d, g * devs + d)
        for g in range(groups)
        for d in range(devs)
    ]


def core_perm(devices):
    return [(i, i ^ 1) for i in range(devices)]


def core_groups(groups, devs, planes):
    blocks = [range(g * devs, (g + 1) * devs) for g in range(groups)]
    if not planes:
        blocks = [range(groups * devs)]
    return [[d for d in b if d % 2 == core] for b in blocks for core in range(2)]


def to_twin(array, devices):
    return lax.ppermute(array, AXES, core_perm(devices))


def from_line(array, groups, devs):
    own = [array] + [
        lax.ppermute(array, AXES, line_perm(groups, devs, d)) for d in range(1, groups)
    ]
    return own + [to_twin(a, groups * devs) for a in own]


def split3(x):
    high = x.astype(jnp.bfloat16)
    rest = x - high.astype(jnp.float32)
    middle = rest.astype(jnp.bfloat16)
    low = (rest - middle.astype(jnp.float32)).astype(jnp.bfloat16)
    return high, middle, low


def tile_body(rows, width, sc, delta, *refs):
    sources = refs[:2]
    parts, blocks, near, far, left, right, block_sem = refs[2:]
    slots = delta.shape[0]
    chunks = width // LANES
    f32, bf16 = jnp.float32, jnp.bfloat16

    def block_copy(s, i, at):
        return pltpu.make_async_copy(sources[s].at[at], blocks.at[i], block_sem.at[i])

    for i in range(2 * slots):
        for s in range(2):
            pl.when(sc[slots + i] == s)(
                lambda i=i, s=s: block_copy(s, i, sc[3 * slots + i]).start()
            )

    for i in range(2 * slots):
        block_copy(0, i, 0).wait()

    parts[2 * slots * DIM * chunks :, :] = jnp.zeros((8, LANES), f32)

    def one_tile(k, _):
        @pl.when(sc[k] > 0)
        def _():
            def spread(i):
                return [blocks[i, c * chunks : (c + 1) * chunks, :] for c in range(DIM)]

            xa, xb = spread(2 * k), spread(2 * k + 1)
            mean = [jnp.sum(a, keepdims=True) * (1.0 / width) for a in xa]
            xa = [a - m for a, m in zip(xa, mean)]
            xb = [b - m for b, m in zip(xb, mean)]

            def fill(ref, x, scale, norm_first):
                pieces = [split3(v) for v in x]
                norm = x[0] * x[0] + x[1] * x[1] + x[2] * x[2]
                norms = split3(norm)
                one = jnp.ones((chunks, LANES), bf16)
                out = []
                for c in range(DIM):
                    for s in range(3):
                        for t in range(3):
                            out.append(pieces[c][s] * scale if norm_first else pieces[c][t])
                for s in range(3):
                    out.append(norms[s] if norm_first else one)
                for s in range(3):
                    out.append(one if norm_first else norms[s])
                return out

            la = fill(None, xa, -2.0, True)
            lb = fill(None, xb, 1.0, False)
            one = jnp.ones((chunks, LANES), bf16)
            va = [p for v in xa for p in split3(v)] + [one]
            vb = [p for v in xb for p in split3(v)] + [one]
            for ref, rows_ in ((left, la), (right, lb), (near, va), (far, vb)):
                ref[...] = jnp.zeros(ref.shape, f32)
                for n, v in enumerate(rows_):
                    v = v.astype(f32)
                    for j in range(chunks):
                        ref[n : n + 1, j * LANES : (j + 1) * LANES] = v[j : j + 1, :]
            cols = right[...].astype(bf16)
            weights = far[...].astype(bf16)

            lhs = jnp.transpose(left[...]).astype(bf16)
            mine = near[...].astype(bf16)
            count = rows // STEP
            pieces = width // DEPTH
            stress = jnp.zeros((16, LANES), f32)
            row, col = [None] * count, [None] * pieces

            def front(n, g):
                lanes = slice(g * DEPTH, (g + 1) * DEPTH)
                return lax.dot_general(
                    lhs[n * STEP : (n + 1) * STEP], cols[:, lanes], (((1,), (0,)), ((), ())), preferred_element_type=f32
                )

            def back(n, g, squared, stress):
                lanes = slice(g * DEPTH, (g + 1) * DEPTH)
                own = mine[:, n * STEP : (n + 1) * STEP]
                own = jnp.concatenate([own, own], axis=1)
                target = delta[k, n * STEP : (n + 1) * STEP, lanes].astype(f32)
                squared = jnp.maximum(squared, FLOOR_SQUARED)
                inverse = lax.rsqrt(squared)
                error = target - squared * inverse
                error = error * error
                for a in range(0, STEP, 16):
                    for b in range(0, DEPTH, LANES):
                        stress = stress + error[a : a + 16, b : b + LANES]
                ratio = target * inverse
                high = ratio.astype(bf16)
                low = (ratio - high.astype(f32)).astype(bf16)
                both = jnp.concatenate([high, low], axis=0)
                return stress, both

            def last(n, g, both):
                lanes = slice(g * DEPTH, (g + 1) * DEPTH)
                own = mine[:, n * STEP : (n + 1) * STEP]
                own = jnp.concatenate([own, own], axis=1)
                a = lax.dot_general(
                    weights[:, lanes], both, (((1,), (1,)), ((), ())), preferred_element_type=f32
                )
                row[n] = a if row[n] is None else row[n] + a
                a = lax.dot_general(own, both, (((1,), (0,)), ((), ())), preferred_element_type=f32)
                col[g] = a if col[g] is None else col[g] + a

            order = [(n, g) for n in range(count) for g in range(pieces)]
            ahead = [front(*order[t]) for t in range(AHEAD)]
            held = []
            for t, (n, g) in enumerate(order):
                if t + AHEAD < len(order):
                    ahead.append(front(*order[t + AHEAD]))
                if len(held) > LAG - 1:
                    last(*held.pop(0))
                stress, both = back(n, g, ahead.pop(0), stress)
                held.append((n, g, both))
            for h in held:
                last(*h)
            row = jnp.concatenate([r[:, :STEP] + r[:, STEP:] for r in row], axis=1)
            col = jnp.concatenate(col, axis=1)
            for side, own, total in ((0, near, row), (1, far, col)):
                for c in range(DIM):
                    cross = total[3 * c : 3 * c + 1] + total[3 * c + 1 : 3 * c + 2] + total[3 * c + 2 : 3 * c + 3]
                    x = own[3 * c : 3 * c + 1, :] + own[3 * c + 1 : 3 * c + 2, :] + own[3 * c + 2 : 3 * c + 3, :]
                    value = x * total[9:10] - cross
                    for j in range(chunks):
                        parts[pl.ds((2 * k + side) * DIM * chunks + c * chunks + j, 1), :] = value[:, j * LANES : (j + 1) * LANES]
            parts[2 * slots * DIM * chunks :, :] += stress[:8] + stress[8:]

        return 0

    lax.fori_loop(0, slots, one_tile, 0)


def fetch_body(source, out, sem):
    copy = pltpu.make_async_copy(source, out, sem)
    copy.start()
    copy.wait()


def fetch(dissim):
    return pl.pallas_call(
        fetch_body,
        out_shape=pltpu.VMEM(dissim.shape, dissim.dtype),
        in_specs=[pl.BlockSpec(memory_space=pl.ANY)],
        out_specs=pl.BlockSpec(memory_space=pltpu.VMEM),
        scratch_shapes=[pltpu.SemaphoreType.DMA],
        cost_estimate=pl.CostEstimate(
            flops=0, bytes_accessed=2 * dissim.size * dissim.dtype.itemsize, transcendentals=0
        ),
        compiler_params=pltpu.CompilerParams(vmem_limit_bytes=8 * 1024 * 1024),
        name="fetch",
    )(dissim)


def tile_parts(scalars, dissim, sources):
    slots, rows, width = dissim.shape
    block_rows = DIM * width // LANES
    return pl.pallas_call(
        functools.partial(tile_body, rows, width),
        out_shape=jax.ShapeDtypeStruct((2 * slots * block_rows + 8, LANES), jnp.float32),
        in_specs=[pl.BlockSpec(memory_space=pltpu.SMEM), pl.BlockSpec(memory_space=pltpu.VMEM)]
        + [pl.BlockSpec(memory_space=pl.ANY)] * 2,
        out_specs=pl.BlockSpec(memory_space=pltpu.VMEM),
        scratch_shapes=[
            pltpu.VMEM((2 * slots, block_rows, LANES), jnp.float32),
            pltpu.VMEM((16, rows), jnp.float32),
            pltpu.VMEM((16, width), jnp.float32),
            pltpu.VMEM((KDIM, rows), jnp.float32),
            pltpu.VMEM((KDIM, width), jnp.float32),
            pltpu.SemaphoreType.DMA((2 * slots,)),
        ],
        compiler_params=pltpu.CompilerParams(vmem_limit_bytes=VMEM_LIMIT),
        name="tile_parts",
    )(scalars, pltpu.with_memory_space_constraint(dissim, pltpu.VMEM), *sources)


def gather_body(count, block_rows, where, *refs):
    sources, out = refs[:-1], refs[-1]
    stress = sources[0][count * block_rows :, :]
    for s in range(1, len(sources)):
        stress = stress + sources[s][count * block_rows :, :]
    for chip in range(out.shape[0]):
        out[chip, :block_rows, :] = jnp.zeros((block_rows, LANES), jnp.float32)
        out[chip, block_rows:, :] = stress
    for s in range(len(sources)):
        for i in range(count):
            chip = where[s * count + i]

            @pl.when(chip >= 0)
            def _(s=s, i=i, chip=chip):
                out[chip, :block_rows, :] += sources[s][
                    i * block_rows : (i + 1) * block_rows, :
                ]


def by_chip(where, sources, chips):
    rows = sources[0].shape[0] - 8
    count = where.shape[0] // len(sources)
    block_rows = rows // count
    return pl.pallas_call(
        functools.partial(gather_body, count, block_rows),
        out_shape=jax.ShapeDtypeStruct((chips, block_rows + 8, LANES), jnp.float32),
        in_specs=[pl.BlockSpec(memory_space=pltpu.SMEM)]
        + [pl.BlockSpec(memory_space=pltpu.VMEM)] * len(sources),
        out_specs=pl.BlockSpec(memory_space=pltpu.VMEM),
        compiler_params=pltpu.CompilerParams(vmem_limit_bytes=VMEM_LIMIT),
        name="by_chip",
    )(where, *sources)


def total_body(width, pieces, out, stress):
    block_rows = pieces.shape[1] - 8
    chunks = width // LANES
    total = pieces[0]
    for i in range(1, pieces.shape[0]):
        total = total + pieces[i]
    for c in range(DIM):
        for j in range(chunks):
            r = c * chunks + j
            out[c : c + 1, j * LANES : (j + 1) * LANES] = total[r : r + 1, :] * (1.0 / width)
    stress[0, 0] = jnp.sum(total[block_rows:, :])


def total_of(pieces, width):
    return pl.pallas_call(
        functools.partial(total_body, width),
        out_shape=(
            jax.ShapeDtypeStruct((DIM, width), jnp.float32),
            jax.ShapeDtypeStruct((1, 1), jnp.float32),
        ),
        in_specs=[pl.BlockSpec(memory_space=pltpu.VMEM)],
        out_specs=(
            pl.BlockSpec(memory_space=pltpu.VMEM),
            pl.BlockSpec(memory_space=pltpu.SMEM),
        ),
        name="total",
    )(pieces)


def tables(tile_list, holder, groups, devs, slots):
    group, dev = lax.axis_index("grp"), lax.axis_index("dev")
    owners = tile_list[:, 2]
    indices = jnp.arange(owners.shape[0], dtype=jnp.int32)
    earlier = (owners[:, None] == owners[None, :]) & (indices[None, :] < indices[:, None])
    rank = jnp.sum(earlier.astype(jnp.int32), axis=1)
    blocks = jnp.arange(holder.shape[0], dtype=jnp.int32)
    position = jnp.sum(
        jnp.where(tile_list[:, :2, None] == blocks, holder, 0), axis=2
    )
    order = jnp.arange(2 * groups, dtype=jnp.int32)
    line = (group + order) % groups * devs + (dev ^ (order // groups))
    wanted = (line[:, None] * slots + jnp.arange(slots, dtype=jnp.int32)).reshape(-1)
    chosen = wanted[:, None] == (owners * slots + rank)[None, :]
    held = jnp.sum(jnp.where(chosen[:, :, None], position + 1, 0), axis=1).reshape(-1) - 1
    mine = held[: 2 * slots]
    present = (mine[::2] >= 0).astype(jnp.int32)
    at = jnp.maximum(mine, 0)
    for_tiles = jnp.concatenate([present, at % 2 ^ dev % 2, at // 2])
    here = (held >= 0) & (held // devs == group) & (held % 2 == dev % 2)
    where = jnp.where(here, held % devs // 2, -1)
    return for_tiles, where


def on_device(tile_list, holder, coordinates, dissim):
    groups, devs = lax.axis_size("grp"), lax.axis_size("dev")
    chips = devs // 2
    width = coordinates.shape[1]
    slots = dissim.shape[0]
    block_rows = DIM * width // LANES
    for_tiles, where = tables(tile_list, holder, groups, devs, slots)
    delta = fetch(dissim)
    sent = jnp.broadcast_to(
        coordinates.reshape(1, block_rows, LANES), (groups * chips, block_rows, LANES)
    )
    own = lax.all_to_all(
        sent, AXES, 0, 0, tiled=True, axis_index_groups=core_groups(groups, devs, False)
    )
    parts = tile_parts(for_tiles, delta, [own, to_twin(own, groups * devs)])
    pieces = by_chip(where, from_line(parts, groups, devs), chips)
    pieces = lax.all_to_all(
        pieces, AXES, 0, 0, tiled=True, axis_index_groups=core_groups(groups, devs, True)
    )
    guttman, stress = total_of(pieces, width)
    return guttman, stress[0, 0]


def solution(mesh):
    placed = (P(), P(), P(None, AXES), P(AXES, None, None))
    return jax.shard_map(
        on_device,
        mesh=mesh,
        in_specs=placed,
        out_specs=(P(None, AXES), P()),
        check_vma=False,
    )
```

```python
import functools

import jax
import jax.numpy as jnp
from jax import lax
from jax.experimental import pallas as pl
from jax.experimental.pallas import tpu as pltpu
from jax.sharding import PartitionSpec as P

AXES = ("grp", "dev")
FLOOR_SQUARED = 0.0625
LANES = 128
DIM = 3
VMEM_LIMIT = 24 * 1024 * 1024
SMALL_LIMIT = 8 * 1024 * 1024
KDIM = 128
STEP = 128
DEPTH = 512
AHEAD = 1
LAG = 1


def line_perm(groups, devs, shift):
    return [
        (((g + shift) % groups) * devs + d, g * devs + d)
        for g in range(groups)
        for d in range(devs)
    ]


def core_perm(devices):
    return [(i, i ^ 1) for i in range(devices)]


def plane_groups(groups, devs):
    return [
        [g * devs + 2 * chip + core for chip in range(devs // 2)]
        for g in range(groups)
        for core in range(2)
    ]


def to_twin(array, devices):
    return lax.ppermute(array, AXES, core_perm(devices))


def from_line(array, groups, devs):
    return [array] + [
        lax.ppermute(array, AXES, line_perm(groups, devs, d)) for d in range(1, groups)
    ]


def spread_body(*refs):
    sources, out = refs[:-1], refs[-1]
    chunks = sources[0].shape[1] // LANES
    rows = [
        s[c : c + 1, j * LANES : (j + 1) * LANES]
        for s in sources
        for c in range(DIM)
        for j in range(chunks)
    ]
    block = jnp.concatenate(rows, axis=0)
    for chip in range(out.shape[0]):
        out[chip] = block


def spread(sources, chips):
    rows = len(sources) * sources[0].size // LANES
    return pl.pallas_call(
        spread_body,
        out_shape=jax.ShapeDtypeStruct((chips, rows, LANES), jnp.float32),
        in_specs=[pl.BlockSpec(memory_space=pltpu.VMEM)] * len(sources),
        out_specs=pl.BlockSpec(memory_space=pltpu.VMEM),
        compiler_params=pltpu.CompilerParams(vmem_limit_bytes=SMALL_LIMIT),
        name="spread",
    )(*sources)


def split3(x):
    high = x.astype(jnp.bfloat16)
    rest = x - high.astype(jnp.float32)
    middle = rest.astype(jnp.bfloat16)
    low = (rest - middle.astype(jnp.float32)).astype(jnp.bfloat16)
    return high, middle, low


def tile_body(rows, width, sc, delta_hbm, *refs):
    sources = refs[:2]
    parts, delta, near, far, left, right, delta_sem = refs[2:]
    slots = delta.shape[0]
    chunks = width // LANES
    f32, bf16 = jnp.float32, jnp.bfloat16

    def delta_copy(k):
        return pltpu.make_async_copy(delta_hbm.at[k], delta.at[k], delta_sem.at[k])

    pl.when(sc[0] > 0)(lambda: delta_copy(0).start())

    parts[2 * slots * DIM * chunks :, :] = jnp.zeros((8, LANES), f32)

    def one_tile(k, _):
        @pl.when(sc[k] > 0)
        def _():
            delta_copy(k).wait()
            later = jnp.minimum(k + 1, slots - 1)
            pl.when((k + 1 < slots) & (sc[later] > 0))(lambda: delta_copy(later).start())

            def spread(i):
                twin, at = sc[slots + i] > 0, sc[3 * slots + i]
                found = jnp.where(twin, sources[1][at], sources[0][at])
                return [found[c * chunks : (c + 1) * chunks, :] for c in range(DIM)]

            xa, xb = spread(2 * k), spread(2 * k + 1)
            mean = [jnp.sum(a, keepdims=True) * (1.0 / width) for a in xa]
            xa = [a - m for a, m in zip(xa, mean)]
            xb = [b - m for b, m in zip(xb, mean)]

            def fill(ref, x, scale, norm_first):
                pieces = [split3(v) for v in x]
                norm = x[0] * x[0] + x[1] * x[1] + x[2] * x[2]
                norms = split3(norm)
                one = jnp.ones((chunks, LANES), bf16)
                out = []
                for c in range(DIM):
                    for s in range(3):
                        for t in range(3):
                            out.append(pieces[c][s] * scale if norm_first else pieces[c][t])
                for s in range(3):
                    out.append(norms[s] if norm_first else one)
                for s in range(3):
                    out.append(one if norm_first else norms[s])
                return out

            la = fill(None, xa, -2.0, True)
            lb = fill(None, xb, 1.0, False)
            one = jnp.ones((chunks, LANES), bf16)
            va = [p for v in xa for p in split3(v)] + [one]
            vb = [p for v in xb for p in split3(v)] + [one]
            for ref, rows_ in ((left, la), (right, lb), (near, va), (far, vb)):
                ref[...] = jnp.zeros(ref.shape, f32)
                for n, v in enumerate(rows_):
                    v = v.astype(f32)
                    for j in range(chunks):
                        ref[n : n + 1, j * LANES : (j + 1) * LANES] = v[j : j + 1, :]
            cols = right[...].astype(bf16)
            weights = far[...].astype(bf16)

            lhs = jnp.transpose(left[...]).astype(bf16)
            mine = near[...].astype(bf16)
            count = rows // STEP
            pieces = width // DEPTH
            stress = jnp.zeros((16, LANES), f32)
            row, col = [None] * count, [None] * pieces

            def front(n, g):
                lanes = slice(g * DEPTH, (g + 1) * DEPTH)
                return lax.dot_general(
                    lhs[n * STEP : (n + 1) * STEP], cols[:, lanes], (((1,), (0,)), ((), ())), preferred_element_type=f32
                )

            def back(n, g, squared, stress):
                lanes = slice(g * DEPTH, (g + 1) * DEPTH)
                own = mine[:, n * STEP : (n + 1) * STEP]
                own = jnp.concatenate([own, own], axis=1)
                target = delta[k, n * STEP : (n + 1) * STEP, lanes].astype(f32)
                squared = jnp.maximum(squared, FLOOR_SQUARED)
                inverse = lax.rsqrt(squared)
                error = target - squared * inverse
                error = error * error
                for a in range(0, STEP, 16):
                    for b in range(0, DEPTH, LANES):
                        stress = stress + error[a : a + 16, b : b + LANES]
                ratio = target * inverse
                high = ratio.astype(bf16)
                low = (ratio - high.astype(f32)).astype(bf16)
                both = jnp.concatenate([high, low], axis=0)
                return stress, both

            def last(n, g, both):
                lanes = slice(g * DEPTH, (g + 1) * DEPTH)
                own = mine[:, n * STEP : (n + 1) * STEP]
                own = jnp.concatenate([own, own], axis=1)
                a = lax.dot_general(
                    weights[:, lanes], both, (((1,), (1,)), ((), ())), preferred_element_type=f32
                )
                row[n] = a if row[n] is None else row[n] + a
                a = lax.dot_general(own, both, (((1,), (0,)), ((), ())), preferred_element_type=f32)
                col[g] = a if col[g] is None else col[g] + a

            order = [(n, g) for n in range(count) for g in range(pieces)]
            ahead = [front(*order[t]) for t in range(AHEAD)]
            held = []
            for t, (n, g) in enumerate(order):
                if t + AHEAD < len(order):
                    ahead.append(front(*order[t + AHEAD]))
                if len(held) > LAG - 1:
                    last(*held.pop(0))
                stress, both = back(n, g, ahead.pop(0), stress)
                held.append((n, g, both))
            for h in held:
                last(*h)
            row = jnp.concatenate([r[:, :STEP] + r[:, STEP:] for r in row], axis=1)
            col = jnp.concatenate(col, axis=1)
            for side, own, total in ((0, near, row), (1, far, col)):
                for c in range(DIM):
                    cross = total[3 * c : 3 * c + 1] + total[3 * c + 1 : 3 * c + 2] + total[3 * c + 2 : 3 * c + 3]
                    x = own[3 * c : 3 * c + 1, :] + own[3 * c + 1 : 3 * c + 2, :] + own[3 * c + 2 : 3 * c + 3, :]
                    value = x * total[9:10] - cross
                    for j in range(chunks):
                        parts[pl.ds((2 * k + side) * DIM * chunks + c * chunks + j, 1), :] = value[:, j * LANES : (j + 1) * LANES]
            parts[2 * slots * DIM * chunks :, :] += stress[:8] + stress[8:]

        return 0

    lax.fori_loop(0, slots, one_tile, 0)


def tile_parts(scalars, dissim, sources):
    slots, rows, width = dissim.shape
    block_rows = DIM * width // LANES
    return pl.pallas_call(
        functools.partial(tile_body, rows, width),
        out_shape=jax.ShapeDtypeStruct((2 * slots * block_rows + 8, LANES), jnp.float32),
    in_specs=[pl.BlockSpec(memory_space=pltpu.SMEM), pl.BlockSpec(memory_space=pltpu.HBM)]
        + [pl.BlockSpec(memory_space=pltpu.VMEM)] * 2,
        out_specs=pl.BlockSpec(memory_space=pltpu.VMEM),
        scratch_shapes=[
            pltpu.VMEM((slots, rows, width), jnp.bfloat16),
            pltpu.VMEM((16, rows), jnp.float32),
            pltpu.VMEM((16, width), jnp.float32),
            pltpu.VMEM((KDIM, rows), jnp.float32),
            pltpu.VMEM((KDIM, width), jnp.float32),
            pltpu.SemaphoreType.DMA((slots,)),
        ],
        compiler_params=pltpu.CompilerParams(vmem_limit_bytes=VMEM_LIMIT),
        name="tile_parts",
    )(scalars, pltpu.with_memory_space_constraint(dissim, pltpu.HBM), *sources)


def gather_body(count, block_rows, where, *refs):
    sources, out = refs[:-1], refs[-1]
    stress = sources[0][count * block_rows :, :]
    for s in range(1, len(sources)):
        stress = stress + sources[s][count * block_rows :, :]
    for chip in range(out.shape[0]):
        out[chip, :block_rows, :] = jnp.zeros((block_rows, LANES), jnp.float32)
        out[chip, block_rows:, :] = stress
    for s in range(len(sources)):
        for i in range(count):
            chip = where[s * count + i]

            @pl.when(chip >= 0)
            def _(s=s, i=i, chip=chip):
                out[chip, :block_rows, :] += sources[s][
                    i * block_rows : (i + 1) * block_rows, :
                ]


def by_chip(where, sources, chips):
    rows = sources[0].shape[0] - 8
    count = where.shape[0] // len(sources)
    block_rows = rows // count
    return pl.pallas_call(
        functools.partial(gather_body, count, block_rows),
        out_shape=jax.ShapeDtypeStruct((chips, block_rows + 8, LANES), jnp.float32),
        in_specs=[pl.BlockSpec(memory_space=pltpu.SMEM)]
        + [pl.BlockSpec(memory_space=pltpu.VMEM)] * len(sources),
        out_specs=pl.BlockSpec(memory_space=pltpu.VMEM),
        compiler_params=pltpu.CompilerParams(vmem_limit_bytes=SMALL_LIMIT),
        name="by_chip",
    )(where, *sources)


def total_body(width, pieces, out, stress):
    block_rows = pieces.shape[1] - 8
    chunks = width // LANES
    total = pieces[0]
    for i in range(1, pieces.shape[0]):
        total = total + pieces[i]
    for c in range(DIM):
        for j in range(chunks):
            r = c * chunks + j
            out[c : c + 1, j * LANES : (j + 1) * LANES] = total[r : r + 1, :] * (1.0 / width)
    stress[0, 0] = jnp.sum(total[block_rows:, :])


def total_of(pieces, width):
    return pl.pallas_call(
        functools.partial(total_body, width),
        out_shape=(
            jax.ShapeDtypeStruct((DIM, width), jnp.float32),
            jax.ShapeDtypeStruct((1, 1), jnp.float32),
        ),
        in_specs=[pl.BlockSpec(memory_space=pltpu.VMEM)],
        out_specs=(
            pl.BlockSpec(memory_space=pltpu.VMEM),
            pl.BlockSpec(memory_space=pltpu.SMEM),
        ),
        compiler_params=pltpu.CompilerParams(vmem_limit_bytes=SMALL_LIMIT),
        name="total",
    )(pieces)


def tables(tile_list, holder, groups, devs, slots):
    group, dev = lax.axis_index("grp"), lax.axis_index("dev")
    owners = tile_list[:, 2]
    indices = jnp.arange(owners.shape[0], dtype=jnp.int32)
    earlier = (owners[:, None] == owners[None, :]) & (indices[None, :] < indices[:, None])
    rank = jnp.sum(earlier.astype(jnp.int32), axis=1)
    blocks = jnp.arange(holder.shape[0], dtype=jnp.int32)
    position = jnp.sum(
        jnp.where(tile_list[:, :2, None] == blocks, holder, 0), axis=2
    )
    order = jnp.arange(2 * groups, dtype=jnp.int32)
    line = (group + order) % groups * devs + (dev ^ (order // groups))
    wanted = (line[:, None] * slots + jnp.arange(slots, dtype=jnp.int32)).reshape(-1)
    chosen = wanted[:, None] == (owners * slots + rank)[None, :]
    held = jnp.sum(jnp.where(chosen[:, :, None], position + 1, 0), axis=1).reshape(-1) - 1
    mine = held[: 2 * slots]
    present = (mine[::2] >= 0).astype(jnp.int32)
    at = jnp.maximum(mine, 0)
    place = at % devs // 2 * groups + (at // devs - group) % groups
    for_tiles = jnp.concatenate([present, at % 2 ^ dev % 2, place])
    here = (held >= 0) & (held // devs == group) & (held % 2 == dev % 2)
    where = jnp.where(here, held % devs // 2, -1)
    return for_tiles, where


def on_device(tile_list, holder, coordinates, dissim):
    groups, devs = lax.axis_size("grp"), lax.axis_size("dev")
    chips = devs // 2
    width = coordinates.shape[1]
    slots = dissim.shape[0]
    block_rows = DIM * width // LANES
    for_tiles, where = tables(tile_list, holder, groups, devs, slots)
    plane = plane_groups(groups, devs)
    sent = spread(from_line(coordinates, groups, devs), chips)
    own = lax.all_to_all(sent, AXES, 0, 0, tiled=True, axis_index_groups=plane)
    own = own.reshape(groups * chips, block_rows, LANES)
    parts = tile_parts(for_tiles, dissim, [own, to_twin(own, groups * devs)])
    line = from_line(parts, groups, devs)
    line = line + [to_twin(a, groups * devs) for a in line]
    pieces = by_chip(where, line, chips)
    pieces = lax.all_to_all(pieces, AXES, 0, 0, tiled=True, axis_index_groups=plane)
    guttman, stress = total_of(pieces, width)
    return guttman, stress[0, 0]


def solution(mesh):
    placed = (P(), P(), P(None, AXES), P(AXES, None, None))
    return jax.shard_map(
        on_device,
        mesh=mesh,
        in_specs=placed,
        out_specs=(P(None, AXES), P()),
        check_vma=False,
    )
```

```python
import functools

import jax
import jax.numpy as jnp
from jax import lax
from jax.experimental import pallas as pl
from jax.experimental.pallas import tpu as pltpu
from jax.sharding import PartitionSpec as P

AXES = ("grp", "dev")
FLOOR_SQUARED = 0.0625
LANES = 128
DIM = 3
VMEM_LIMIT = 24 * 1024 * 1024
SMALL_LIMIT = 8 * 1024 * 1024
KDIM = 48
STEP = 128
DEPTH = 256
AHEAD = 6
LAG = 2


def line_perm(groups, devs, shift):
    return [
        (((g + shift) % groups) * devs + d, g * devs + d)
        for g in range(groups)
        for d in range(devs)
    ]


def core_perm(devices):
    return [(i, i ^ 1) for i in range(devices)]


def plane_groups(groups, devs):
    return [
        [g * devs + 2 * chip + core for chip in range(devs // 2)]
        for g in range(groups)
        for core in range(2)
    ]


def to_twin(array, devices):
    return lax.ppermute(array, AXES, core_perm(devices))


def from_line(array, groups, devs):
    return [array] + [
        lax.ppermute(array, AXES, line_perm(groups, devs, d)) for d in range(1, groups)
    ]


def spread_body(*refs):
    sources, out = refs[:-1], refs[-1]
    chunks = sources[1].shape[1] // LANES
    rows = [
        s[c : c + 1, j * LANES : (j + 1) * LANES]
        for s in sources[1:]
        for c in range(DIM)
        for j in range(chunks)
    ]
    block = jnp.concatenate([sources[0][...]] + rows, axis=0)
    for chip in range(out.shape[0]):
        out[chip] = block


def spread(sources, chips):
    rows = len(sources) * sources[0].size // LANES
    return pl.pallas_call(
        spread_body,
        out_shape=jax.ShapeDtypeStruct((chips, rows, LANES), jnp.float32),
        in_specs=[pl.BlockSpec(memory_space=pltpu.VMEM)] * len(sources),
        out_specs=pl.BlockSpec(memory_space=pltpu.VMEM),
        compiler_params=pltpu.CompilerParams(vmem_limit_bytes=SMALL_LIMIT),
        name="spread",
    )(*sources)


def split3(x):
    high = x.astype(jnp.bfloat16).astype(jnp.float32)
    rest = x - high
    middle = rest.astype(jnp.bfloat16).astype(jnp.float32)
    low = (rest - middle).astype(jnp.bfloat16).astype(jnp.float32)
    return high, middle, low


def tile_body(rows, width, sc, delta_hbm, first, *refs):
    sources = refs[:2]
    parts, delta, near, far, left, right, delta_sem = refs[2:]
    slots = delta.shape[0]
    chunks = width // LANES
    f32, bf16 = jnp.float32, jnp.bfloat16

    def delta_copy(k):
        return pltpu.make_async_copy(delta_hbm.at[k], delta.at[k], delta_sem.at[k])

    @pl.when(sc[0] > 0)
    def _():
        pltpu.make_async_copy(first, delta.at[0], delta_sem.at[0]).start()


    parts[2 * slots * DIM * chunks :, :] = jnp.zeros((8, LANES), f32)
    for ref in (near, far, left, right):
        ref[...] = jnp.zeros(ref.shape, f32)

    def one_tile(k, _):
        @pl.when(sc[k] > 0)
        def _():
            delta_copy(k).wait()
            later = jnp.minimum(k + 1, slots - 1)
            pl.when((k + 1 < slots) & (sc[later] > 0))(lambda: delta_copy(later).start())

            def block(i):
                twin, at = sc[slots + i] > 0, sc[3 * slots + i]
                found = jnp.where(twin, sources[1][at], sources[0][at])
                return [found[c * chunks : (c + 1) * chunks, :] for c in range(DIM)]

            xa, xb = block(2 * k), block(2 * k + 1)
            mean = [jnp.sum(a, keepdims=True) * (1.0 / width) for a in xa]
            xa = [a - m for a, m in zip(xa, mean)]
            xb = [b - m for b, m in zip(xb, mean)]
            one = jnp.ones((chunks, LANES), f32)

            def terms(x):
                pieces = [split3(v) for v in x]
                norms = split3(x[0] * x[0] + x[1] * x[1] + x[2] * x[2])
                return pieces, list(norms)

            (pa, na), (pb, nb) = terms(xa), terms(xb)
            pairs = [(s, t) for s in range(3) for t in range(3)]
            la = [p[s] * -2.0 for p in pa for s, _ in pairs] + na + [one] * 3
            lb = [p[t] for p in pb for _, t in pairs] + [one] * 3 + nb
            va = [v for p in pa for v in p] + [one]
            vb = [v for p in pb for v in p] + [one]
            for ref, values in ((left, la), (right, lb), (near, va), (far, vb)):
                for n, v in enumerate(values):
                    ref[n] = v
            count = rows // STEP
            pieces = width // DEPTH

            def wide(ref, g):
                each = DEPTH // LANES
                return jnp.concatenate(
                    [ref[:, g * each + e, :] for e in range(each)], axis=1
                ).astype(bf16)

            lhs = [jnp.transpose(left[:, n, :]).astype(bf16) for n in range(count)]
            mine = [near[:, n, :].astype(bf16) for n in range(count)]
            mine = [jnp.concatenate([m, m], axis=1) for m in mine]
            cols = [wide(right, g) for g in range(pieces)]
            weights = [wide(far, g) for g in range(pieces)]
            stress = jnp.zeros((16, LANES), f32)
            row, col = [None] * count, [None] * pieces

            def front(n, g):
                return lax.dot_general(
                    lhs[n], cols[g], (((1,), (0,)), ((), ())), preferred_element_type=f32
                )

            def back(n, g, squared, stress):
                lanes = slice(g * DEPTH, (g + 1) * DEPTH)
                target = delta[k, n * STEP : (n + 1) * STEP, lanes].astype(f32)
                squared = jnp.maximum(squared, FLOOR_SQUARED)
                inverse = lax.rsqrt(squared)
                error = target - squared * inverse
                error = error * error
                for a in range(0, STEP, 16):
                    for b in range(0, DEPTH, LANES):
                        stress = stress + error[a : a + 16, b : b + LANES]
                ratio = target * inverse
                high = ratio.astype(bf16)
                low = (ratio - high.astype(f32)).astype(bf16)
                return stress, jnp.concatenate([high, low], axis=0)

            def last(n, g, both):
                a = lax.dot_general(
                    mine[n], both, (((1,), (0,)), ((), ())), preferred_element_type=f32
                )
                col[g] = a if col[g] is None else col[g] + a
                a = lax.dot_general(
                    weights[g], both, (((1,), (1,)), ((), ())), preferred_element_type=f32
                )
                row[n] = a if row[n] is None else row[n] + a

            order = [(n, g) for n in range(count) for g in range(pieces)]
            ahead = [front(*order[t]) for t in range(AHEAD)]
            held = []
            for t, (n, g) in enumerate(order):
                if t + AHEAD < len(order):
                    ahead.append(front(*order[t + AHEAD]))
                if len(held) > LAG - 1:
                    last(*held.pop(0))
                stress, both = back(n, g, ahead.pop(0), stress)
                held.append((n, g, both))
            for h in held:
                last(*h)
            row = [r[:, :STEP] + r[:, STEP:] for r in row]
            col = [c[:, e * LANES : (e + 1) * LANES] for c in col for e in range(DEPTH // LANES)]
            for side, own, total in ((0, xa, row), (1, xb, col)):
                first_row = (2 * k + side) * DIM * chunks
                for c in range(DIM):
                    for j in range(chunks):
                        t = total[j]
                        cross = t[3 * c : 3 * c + 1] + t[3 * c + 1 : 3 * c + 2] + t[3 * c + 2 : 3 * c + 3]
                        value = own[c][j : j + 1] * t[9:10] - cross
                        parts[pl.ds(first_row + c * chunks + j, 1), :] = value
            parts[2 * slots * DIM * chunks :, :] += stress[:8] + stress[8:]

        return 0

    lax.fori_loop(0, slots, one_tile, 0)


def fetch_body(source, out, sem):
    copy = pltpu.make_async_copy(source.at[0], out, sem)
    copy.start()
    copy.wait()


def first_tile(dissim):
    return pl.pallas_call(
        fetch_body,
        out_shape=pltpu.VMEM(dissim.shape[1:], dissim.dtype),
        in_specs=[pl.BlockSpec(memory_space=pltpu.HBM)],
        out_specs=pl.BlockSpec(memory_space=pltpu.VMEM),
        scratch_shapes=[pltpu.SemaphoreType.DMA],
        compiler_params=pltpu.CompilerParams(vmem_limit_bytes=SMALL_LIMIT),
        name="first_tile",
    )(pltpu.with_memory_space_constraint(dissim, pltpu.HBM))


def tile_parts(scalars, dissim, first, sources):
    slots, rows, width = dissim.shape
    block_rows = DIM * width // LANES
    return pl.pallas_call(
        functools.partial(tile_body, rows, width),
        out_shape=jax.ShapeDtypeStruct((2 * slots * block_rows + 8, LANES), jnp.float32),
    in_specs=[pl.BlockSpec(memory_space=pltpu.SMEM), pl.BlockSpec(memory_space=pltpu.HBM)]
        + [pl.BlockSpec(memory_space=pltpu.VMEM)] * 3,
        out_specs=pl.BlockSpec(memory_space=pltpu.VMEM),
        scratch_shapes=[
            pltpu.VMEM((slots, rows, width), jnp.bfloat16),
            pltpu.VMEM((16, rows // LANES, LANES), jnp.float32),
            pltpu.VMEM((16, width // LANES, LANES), jnp.float32),
            pltpu.VMEM((KDIM, rows // LANES, LANES), jnp.float32),
            pltpu.VMEM((KDIM, width // LANES, LANES), jnp.float32),
            pltpu.SemaphoreType.DMA((slots,)),
        ],
        compiler_params=pltpu.CompilerParams(vmem_limit_bytes=VMEM_LIMIT),
        name="tile_parts",
    )(
        scalars,
        pltpu.with_memory_space_constraint(dissim, pltpu.HBM),
        pltpu.with_memory_space_constraint(first, pltpu.VMEM),
        *sources,
    )


def gather_body(count, block_rows, where, *refs):
    sources, out = refs[:-1], refs[-1]
    stress = sources[0][count * block_rows :, :]
    for s in range(1, len(sources)):
        stress = stress + sources[s][count * block_rows :, :]
    for chip in range(out.shape[0]):
        out[chip, :block_rows, :] = jnp.zeros((block_rows, LANES), jnp.float32)
        out[chip, block_rows:, :] = stress
    for s in range(len(sources)):
        for i in range(count):
            chip = where[s * count + i]

            @pl.when(chip >= 0)
            def _(s=s, i=i, chip=chip):
                out[chip, :block_rows, :] += sources[s][
                    i * block_rows : (i + 1) * block_rows, :
                ]


def by_chip(where, sources, chips):
    rows = sources[0].shape[0] - 8
    count = where.shape[0] // len(sources)
    block_rows = rows // count
    return pl.pallas_call(
        functools.partial(gather_body, count, block_rows),
        out_shape=jax.ShapeDtypeStruct((chips, block_rows + 8, LANES), jnp.float32),
        in_specs=[pl.BlockSpec(memory_space=pltpu.SMEM)]
        + [pl.BlockSpec(memory_space=pltpu.VMEM)] * len(sources),
        out_specs=pl.BlockSpec(memory_space=pltpu.VMEM),
        compiler_params=pltpu.CompilerParams(vmem_limit_bytes=SMALL_LIMIT),
        name="by_chip",
    )(where, *sources)


def total_body(width, pieces, out, stress):
    block_rows = pieces.shape[1] - 8
    chunks = width // LANES
    total = pieces[0]
    for i in range(1, pieces.shape[0]):
        total = total + pieces[i]
    for c in range(DIM):
        for j in range(chunks):
            r = c * chunks + j
            out[c : c + 1, j * LANES : (j + 1) * LANES] = total[r : r + 1, :] * (1.0 / width)
    stress[0, 0] = jnp.sum(total[block_rows:, :])


def total_of(pieces, width):
    return pl.pallas_call(
        functools.partial(total_body, width),
        out_shape=(
            jax.ShapeDtypeStruct((DIM, width), jnp.float32),
            jax.ShapeDtypeStruct((1, 1), jnp.float32),
        ),
        in_specs=[pl.BlockSpec(memory_space=pltpu.VMEM)],
        out_specs=(
            pl.BlockSpec(memory_space=pltpu.VMEM),
            pl.BlockSpec(memory_space=pltpu.SMEM),
        ),
        compiler_params=pltpu.CompilerParams(vmem_limit_bytes=SMALL_LIMIT),
        name="total",
    )(pieces)


def tables(tile_list, holder, groups, devs, slots):
    group, dev = lax.axis_index("grp"), lax.axis_index("dev")
    owners = tile_list[:, 2]
    indices = jnp.arange(owners.shape[0], dtype=jnp.int32)
    earlier = (owners[:, None] == owners[None, :]) & (indices[None, :] < indices[:, None])
    rank = jnp.sum(earlier.astype(jnp.int32), axis=1)
    blocks = jnp.arange(holder.shape[0], dtype=jnp.int32)
    position = jnp.sum(
        jnp.where(tile_list[:, :2, None] == blocks, holder, 0), axis=2
    )
    order = jnp.arange(2 * groups, dtype=jnp.int32)
    line = (group + order) % groups * devs + (dev ^ (order // groups))
    wanted = (line[:, None] * slots + jnp.arange(slots, dtype=jnp.int32)).reshape(-1)
    chosen = wanted[:, None] == (owners * slots + rank)[None, :]
    held = jnp.sum(jnp.where(chosen[:, :, None], position + 1, 0), axis=1).reshape(-1) - 1
    mine = held[: 2 * slots]
    present = (mine[::2] >= 0).astype(jnp.int32)
    at = jnp.maximum(mine, 0)
    place = at % devs // 2 * groups + (at // devs - group) % groups
    for_tiles = jnp.concatenate([present, at % 2 ^ dev % 2, place])
    here = (held >= 0) & (held // devs == group) & (held % 2 == dev % 2)
    where = jnp.where(here, held % devs // 2, -1)
    return for_tiles, where


def on_device(tile_list, holder, coordinates, dissim):
    groups, devs = lax.axis_size("grp"), lax.axis_size("dev")
    chips = devs // 2
    width = coordinates.shape[1]
    slots = dissim.shape[0]
    block_rows = DIM * width // LANES
    for_tiles, where = tables(tile_list, holder, groups, devs, slots)
    plane = plane_groups(groups, devs)
    line = from_line(coordinates, groups, devs)
    line[0] = coordinates.reshape(block_rows, LANES)
    sent = spread(line, chips)
    own = lax.all_to_all(sent, AXES, 0, 0, tiled=True, axis_index_groups=plane)
    own, dissim = lax.optimization_barrier((own, dissim))
    own = own.reshape(groups * chips, block_rows, LANES)
    twin = to_twin(own, groups * devs)
    parts = tile_parts(for_tiles, dissim, first_tile(dissim), [own, twin])
    line = from_line(parts, groups, devs)
    line = line + [to_twin(a, groups * devs) for a in line]
    pieces = by_chip(where, line, chips)
    pieces = lax.all_to_all(pieces, AXES, 0, 0, tiled=True, axis_index_groups=plane)
    guttman, stress = total_of(pieces, width)
    return guttman, stress[0, 0]


def solution(mesh):
    placed = (P(), P(), P(None, AXES), P(AXES, None, None))
    return jax.shard_map(
        on_device,
        mesh=mesh,
        in_specs=placed,
        out_specs=(P(None, AXES), P()),
        check_vma=False,
    )
```

```python
import functools

import jax
import jax.numpy as jnp
from jax import lax
from jax.experimental import pallas as pl
from jax.experimental.pallas import tpu as pltpu
from jax.sharding import PartitionSpec as P

AXES = ("grp", "dev")
FLOOR_SQUARED = 0.0625
LANES = 128
DIM = 3
VMEM_LIMIT = 24 * 1024 * 1024
SMALL_LIMIT = 8 * 1024 * 1024
KDIM = 48
STEP = 128
DEPTH = 256
AHEAD = 6
LAG = 2


def line_perm(groups, devs, shift):
    return [
        (((g + shift) % groups) * devs + d, g * devs + d)
        for g in range(groups)
        for d in range(devs)
    ]


def core_perm(devices):
    return [(i, i ^ 1) for i in range(devices)]


def plane_groups(groups, devs):
    return [
        [g * devs + 2 * chip + core for chip in range(devs // 2)]
        for g in range(groups)
        for core in range(2)
    ]


def to_twin(array, devices):
    return lax.ppermute(array, AXES, core_perm(devices))


def from_line(array, groups, devs):
    return [array] + [
        lax.ppermute(array, AXES, line_perm(groups, devs, d)) for d in range(1, groups)
    ]


def spread_body(*refs):
    sources, out = refs[:-1], refs[-1]
    chunks = sources[1].shape[1] // LANES
    rows = [
        s[c : c + 1, j * LANES : (j + 1) * LANES]
        for s in sources[1:]
        for c in range(DIM)
        for j in range(chunks)
    ]
    block = jnp.concatenate([sources[0][...]] + rows, axis=0)
    for chip in range(out.shape[0]):
        out[chip] = block


def spread(sources, chips):
    rows = len(sources) * sources[0].size // LANES
    return pl.pallas_call(
        spread_body,
        out_shape=jax.ShapeDtypeStruct((chips, rows, LANES), jnp.float32),
        in_specs=[pl.BlockSpec(memory_space=pltpu.VMEM)] * len(sources),
        out_specs=pl.BlockSpec(memory_space=pltpu.VMEM),
        compiler_params=pltpu.CompilerParams(vmem_limit_bytes=SMALL_LIMIT),
        name="spread",
    )(*sources)


def split3(x):
    high = x.astype(jnp.bfloat16).astype(jnp.float32)
    rest = x - high
    middle = rest.astype(jnp.bfloat16).astype(jnp.float32)
    low = (rest - middle).astype(jnp.bfloat16).astype(jnp.float32)
    return high, middle, low


def tile_body(rows, width, sc, delta_hbm, first, *refs):
    sources = refs[:2]
    parts, delta, near, far, left, right, delta_sem = refs[2:]
    slots = delta.shape[0]
    chunks = width // LANES
    f32, bf16 = jnp.float32, jnp.bfloat16

    def delta_copy(k):
        return pltpu.make_async_copy(delta_hbm.at[k], delta.at[k], delta_sem.at[k])

    @pl.when(sc[6, 0] > 0)
    def _():
        pltpu.make_async_copy(first, delta.at[0], delta_sem.at[0]).start()


    parts[2 * slots * DIM * chunks :, :] = jnp.zeros((8, LANES), f32)
    for ref in (near, far, left, right):
        ref[...] = jnp.zeros(ref.shape, f32)

    def one_tile(k, _):
        @pl.when(sc[6, k] > 0)
        def _():
            delta_copy(k).wait()
            later = jnp.minimum(k + 1, slots - 1)
            pl.when((k + 1 < slots) & (sc[6, later] > 0))(lambda: delta_copy(later).start())

            def block(side):
                twin, at = sc[4 + side, k] > 0, sc[side, k]
                found = jnp.where(twin, sources[1][at], sources[0][at])
                return [found[c * chunks : (c + 1) * chunks, :] for c in range(DIM)]

            xa, xb = block(0), block(1)
            mean = [jnp.sum(a, keepdims=True) * (1.0 / width) for a in xa]
            xa = [a - m for a, m in zip(xa, mean)]
            xb = [b - m for b, m in zip(xb, mean)]
            one = jnp.ones((chunks, LANES), f32)

            def terms(x):
                pieces = [split3(v) for v in x]
                norms = split3(x[0] * x[0] + x[1] * x[1] + x[2] * x[2])
                return pieces, list(norms)

            (pa, na), (pb, nb) = terms(xa), terms(xb)
            pairs = [(s, t) for s in range(3) for t in range(3)]
            la = [p[s] * -2.0 for p in pa for s, _ in pairs] + na + [one] * 3
            lb = [p[t] for p in pb for _, t in pairs] + [one] * 3 + nb
            va = [v for p in pa for v in p] + [one]
            vb = [v for p in pb for v in p] + [one]
            for ref, values in ((left, la), (right, lb), (near, va), (far, vb)):
                for n, v in enumerate(values):
                    ref[n] = v
            count = rows // STEP
            pieces = width // DEPTH

            def wide(ref, g):
                each = DEPTH // LANES
                return jnp.concatenate(
                    [ref[:, g * each + e, :] for e in range(each)], axis=1
                ).astype(bf16)

            lhs = [jnp.transpose(left[:, n, :]).astype(bf16) for n in range(count)]
            mine = [near[:, n, :].astype(bf16) for n in range(count)]
            mine = [jnp.concatenate([m, m], axis=1) for m in mine]
            cols = [wide(right, g) for g in range(pieces)]
            weights = [wide(far, g) for g in range(pieces)]
            stress = jnp.zeros((16, LANES), f32)
            row, col = [None] * count, [None] * pieces

            def front(n, g):
                return lax.dot_general(
                    lhs[n], cols[g], (((1,), (0,)), ((), ())), preferred_element_type=f32
                )

            def back(n, g, squared, stress):
                lanes = slice(g * DEPTH, (g + 1) * DEPTH)
                target = delta[k, n * STEP : (n + 1) * STEP, lanes].astype(f32)
                squared = jnp.maximum(squared, FLOOR_SQUARED)
                inverse = lax.rsqrt(squared)
                error = target - squared * inverse
                error = error * error
                for a in range(0, STEP, 16):
                    for b in range(0, DEPTH, LANES):
                        stress = stress + error[a : a + 16, b : b + LANES]
                ratio = target * inverse
                high = ratio.astype(bf16)
                low = (ratio - high.astype(f32)).astype(bf16)
                return stress, jnp.concatenate([high, low], axis=0)

            def last(n, g, both):
                a = lax.dot_general(
                    mine[n], both, (((1,), (0,)), ((), ())), preferred_element_type=f32
                )
                col[g] = a if col[g] is None else col[g] + a
                a = lax.dot_general(
                    weights[g], both, (((1,), (1,)), ((), ())), preferred_element_type=f32
                )
                row[n] = a if row[n] is None else row[n] + a

            order = [(n, g) for n in range(count) for g in range(pieces)]
            ahead = [front(*order[t]) for t in range(AHEAD)]
            held = []
            for t, (n, g) in enumerate(order):
                if t + AHEAD < len(order):
                    ahead.append(front(*order[t + AHEAD]))
                if len(held) > LAG - 1:
                    last(*held.pop(0))
                stress, both = back(n, g, ahead.pop(0), stress)
                held.append((n, g, both))
            for h in held:
                last(*h)
            row = [r[:, :STEP] + r[:, STEP:] for r in row]
            col = [c[:, e * LANES : (e + 1) * LANES] for c in col for e in range(DEPTH // LANES)]
            for side, own, total in ((0, xa, row), (1, xb, col)):
                first_row = (2 * k + side) * DIM * chunks
                for c in range(DIM):
                    for j in range(chunks):
                        t = total[j]
                        cross = t[3 * c : 3 * c + 1] + t[3 * c + 1 : 3 * c + 2] + t[3 * c + 2 : 3 * c + 3]
                        value = own[c][j : j + 1] * t[9:10] - cross
                        parts[pl.ds(first_row + c * chunks + j, 1), :] = value
            parts[2 * slots * DIM * chunks :, :] += stress[:8] + stress[8:]

        return 0

    lax.fori_loop(0, slots, one_tile, 0)


def fetch_body(source, out, sem):
    copy = pltpu.make_async_copy(source.at[0], out, sem)
    copy.start()
    copy.wait()


def first_tile(dissim):
    return pl.pallas_call(
        fetch_body,
        out_shape=pltpu.VMEM(dissim.shape[1:], dissim.dtype),
        in_specs=[pl.BlockSpec(memory_space=pltpu.HBM)],
        out_specs=pl.BlockSpec(memory_space=pltpu.VMEM),
        scratch_shapes=[pltpu.SemaphoreType.DMA],
        compiler_params=pltpu.CompilerParams(vmem_limit_bytes=SMALL_LIMIT),
        name="first_tile",
    )(pltpu.with_memory_space_constraint(dissim, pltpu.HBM))


def tile_parts(scalars, dissim, first, sources):
    slots, rows, width = dissim.shape
    block_rows = DIM * width // LANES
    return pl.pallas_call(
        functools.partial(tile_body, rows, width),
        out_shape=jax.ShapeDtypeStruct((2 * slots * block_rows + 8, LANES), jnp.float32),
    in_specs=[pl.BlockSpec(memory_space=pltpu.SMEM), pl.BlockSpec(memory_space=pltpu.HBM)]
        + [pl.BlockSpec(memory_space=pltpu.VMEM)] * 3,
        out_specs=pl.BlockSpec(memory_space=pltpu.VMEM),
        scratch_shapes=[
            pltpu.VMEM((slots, rows, width), jnp.bfloat16),
            pltpu.VMEM((16, rows // LANES, LANES), jnp.float32),
            pltpu.VMEM((16, width // LANES, LANES), jnp.float32),
            pltpu.VMEM((KDIM, rows // LANES, LANES), jnp.float32),
            pltpu.VMEM((KDIM, width // LANES, LANES), jnp.float32),
            pltpu.SemaphoreType.DMA((slots,)),
        ],
        compiler_params=pltpu.CompilerParams(vmem_limit_bytes=VMEM_LIMIT),
        name="tile_parts",
    )(
        scalars,
        pltpu.with_memory_space_constraint(dissim, pltpu.HBM),
        pltpu.with_memory_space_constraint(first, pltpu.VMEM),
        *sources,
    )


def gather_body(count, block_rows, where, *refs):
    sources, out = refs[:-1], refs[-1]
    stress = sources[0][count * block_rows :, :]
    for s in range(1, len(sources)):
        stress = stress + sources[s][count * block_rows :, :]
    for chip in range(out.shape[0]):
        out[chip, :block_rows, :] = jnp.zeros((block_rows, LANES), jnp.float32)
        out[chip, block_rows:, :] = stress
    for s in range(len(sources)):
        for i in range(count):
            chip = where[2 + i % 2, s * (count // 2) + i // 2]

            @pl.when(chip >= 0)
            def _(s=s, i=i, chip=chip):
                out[chip, :block_rows, :] += sources[s][
                    i * block_rows : (i + 1) * block_rows, :
                ]


def by_chip(where, sources, chips, slots):
    rows = sources[0].shape[0] - 8
    count = 2 * slots
    block_rows = rows // count
    return pl.pallas_call(
        functools.partial(gather_body, count, block_rows),
        out_shape=jax.ShapeDtypeStruct((chips, block_rows + 8, LANES), jnp.float32),
        in_specs=[pl.BlockSpec(memory_space=pltpu.SMEM)]
        + [pl.BlockSpec(memory_space=pltpu.VMEM)] * len(sources),
        out_specs=pl.BlockSpec(memory_space=pltpu.VMEM),
        compiler_params=pltpu.CompilerParams(vmem_limit_bytes=SMALL_LIMIT),
        name="by_chip",
    )(where, *sources)


def total_body(width, pieces, out, stress):
    block_rows = pieces.shape[1] - 8
    chunks = width // LANES
    total = pieces[0]
    for i in range(1, pieces.shape[0]):
        total = total + pieces[i]
    for c in range(DIM):
        for j in range(chunks):
            r = c * chunks + j
            out[c : c + 1, j * LANES : (j + 1) * LANES] = total[r : r + 1, :] * (1.0 / width)
    stress[0, 0] = jnp.sum(total[block_rows:, :])


def total_of(pieces, width):
    return pl.pallas_call(
        functools.partial(total_body, width),
        out_shape=(
            jax.ShapeDtypeStruct((DIM, width), jnp.float32),
            jax.ShapeDtypeStruct((1, 1), jnp.float32),
        ),
        in_specs=[pl.BlockSpec(memory_space=pltpu.VMEM)],
        out_specs=(
            pl.BlockSpec(memory_space=pltpu.VMEM),
            pl.BlockSpec(memory_space=pltpu.SMEM),
        ),
        compiler_params=pltpu.CompilerParams(vmem_limit_bytes=SMALL_LIMIT),
        name="total",
    )(pieces)


def tables_body(groups, devs, slots, tiles_hbm, holder_hbm, coords_hbm, out, own, *scratch):
    tiles, holder, coords, sem = scratch
    copies = [
        pltpu.make_async_copy(source, target, sem.at[i])
        for i, (source, target) in enumerate(
            ((tiles_hbm, tiles), (holder_hbm, holder), (coords_hbm, coords))
        )
    ]
    for copy in copies:
        copy.start()
    for copy in copies:
        copy.wait()
    chunks = coords.shape[1] // LANES
    for c in range(DIM):
        for j in range(chunks):
            own[c * chunks + j : c * chunks + j + 1, :] = coords[
                c : c + 1, j * LANES : (j + 1) * LANES
            ]
    f32, i32 = jnp.float32, jnp.int32
    group, dev = lax.axis_index("grp"), lax.axis_index("dev")
    count, blocks = tiles.shape[1], holder.shape[1]
    bits = devs.bit_length() - 1

    def column(row):
        return jnp.transpose(jnp.broadcast_to(row, (LANES, count)))[:, :1]

    owner = column(tiles[2:3, :])
    same = owner == tiles[2:3, :]
    later = lax.broadcasted_iota(i32, (count, count), 0) > lax.broadcasted_iota(
        i32, (count, count), 1
    )
    rank = jnp.sum(jnp.where(same & later, 1.0, 0.0), axis=1, keepdims=True)
    code = owner.astype(f32) * slots + rank
    lane = lax.broadcasted_iota(i32, (1, LANES), 1)
    order = lane // slots
    line = ((group + order) & (groups - 1)) * devs + (dev ^ (order // groups))
    wanted = (line * slots + (lane & (slots - 1))).astype(f32)
    chosen = (code == wanted) & (lane < 2 * groups * slots)
    numbers = lax.broadcasted_iota(i32, (count, blocks), 1)
    places = holder[...].astype(f32) + 1.0
    rows = []
    for side in range(2):
        found = jnp.where(column(tiles[side : side + 1, :]) == numbers, places, 0.0)
        found = jnp.sum(found, axis=1, keepdims=True)
        rows.append(jnp.sum(jnp.where(chosen, found, 0.0), axis=0, keepdims=True))
    held = [r.astype(i32) - 1 for r in rows]
    at = [jnp.maximum(h, 0) for h in held]
    chip = [(a & (devs - 1)) >> 1 for a in at]
    from_group = [(a >> bits) - group & (groups - 1) for a in at]
    twin = [(a ^ dev) & 1 for a in at]
    for side in range(2):
        here = (held[side] >= 0) & (from_group[side] == 0) & (twin[side] == 0)
        out[side : side + 1, :] = chip[side] * groups + from_group[side]
        out[2 + side : 3 + side, :] = jnp.where(here, chip[side], -1)
        out[4 + side : 5 + side, :] = twin[side]
    out[6:7, :] = jnp.where(held[0] >= 0, 1, 0)
    out[7:8, :] = jnp.zeros((1, LANES), i32)


def tables(tile_list, holder, coordinates, groups, devs, slots):
    arrays = [tile_list.T, holder.reshape(1, -1), coordinates]
    return pl.pallas_call(
        functools.partial(tables_body, groups, devs, slots),
        out_shape=(
            jax.ShapeDtypeStruct((8, LANES), jnp.int32),
            jax.ShapeDtypeStruct((coordinates.size // LANES, LANES), jnp.float32),
        ),
        in_specs=[pl.BlockSpec(memory_space=pltpu.HBM)] * 3,
        out_specs=[pl.BlockSpec(memory_space=pltpu.VMEM)] * 2,
        scratch_shapes=[pltpu.VMEM(a.shape, a.dtype) for a in arrays]
        + [pltpu.SemaphoreType.DMA((3,))],
        compiler_params=pltpu.CompilerParams(vmem_limit_bytes=SMALL_LIMIT),
        name="tables",
    )(*[pltpu.with_memory_space_constraint(a, pltpu.HBM) for a in arrays])


def on_device(tile_list, holder, coordinates, dissim):
    groups, devs = lax.axis_size("grp"), lax.axis_size("dev")
    chips = devs // 2
    width = coordinates.shape[1]
    slots = dissim.shape[0]
    block_rows = DIM * width // LANES
    places, rows = tables(tile_list, holder, coordinates, groups, devs, slots)
    plane = plane_groups(groups, devs)
    line = from_line(coordinates, groups, devs)
    line[0] = rows
    sent = spread(line, chips)
    own = lax.all_to_all(sent, AXES, 0, 0, tiled=True, axis_index_groups=plane)
    own, dissim = lax.optimization_barrier((own, dissim))
    own = own.reshape(groups * chips, block_rows, LANES)
    twin = to_twin(own, groups * devs)
    parts = tile_parts(places, dissim, first_tile(dissim), [own, twin])
    line = from_line(parts, groups, devs)
    line = line + [to_twin(a, groups * devs) for a in line]
    pieces = by_chip(places, line, chips, slots)
    pieces = lax.all_to_all(pieces, AXES, 0, 0, tiled=True, axis_index_groups=plane)
    guttman, stress = total_of(pieces, width)
    return guttman, stress[0, 0]


def solution(mesh):
    placed = (P(), P(), P(None, AXES), P(AXES, None, None))
    return jax.shard_map(
        on_device,
        mesh=mesh,
        in_specs=placed,
        out_specs=(P(None, AXES), P()),
        check_vma=False,
    )
```

```python
import functools

import jax
import jax.numpy as jnp
from jax import lax
from jax.experimental import pallas as pl
from jax.experimental.pallas import tpu as pltpu
from jax.sharding import PartitionSpec as P

AXES = ("grp", "dev")
FLOOR_SQUARED = 0.0625
LANES = 128
DIM = 3
VMEM_LIMIT = 24 * 1024 * 1024
SMALL_LIMIT = 8 * 1024 * 1024
KDIM = 48
STEP = 128
DEPTH = 256
AHEAD = 6
LAG = 2


def line_perm(groups, devs, shift):
    return [
        (((g + shift) % groups) * devs + d, g * devs + d)
        for g in range(groups)
        for d in range(devs)
    ]


def core_perm(devices):
    return [(i, i ^ 1) for i in range(devices)]


def plane_groups(groups, devs):
    return [
        [g * devs + 2 * chip + core for chip in range(devs // 2)]
        for g in range(groups)
        for core in range(2)
    ]


def to_twin(array, devices):
    return lax.ppermute(array, AXES, core_perm(devices))


def from_line(array, groups, devs):
    return [array] + [
        lax.ppermute(array, AXES, line_perm(groups, devs, d)) for d in range(1, groups)
    ]


def spread_body(coords, out):
    rows = [
        coords[c : c + 1, j * LANES : (j + 1) * LANES]
        for c in range(DIM)
        for j in range(coords.shape[1] // LANES)
    ]
    block = jnp.concatenate(rows, axis=0)
    for chip in range(out.shape[0]):
        out[chip] = block


def spread(coordinates, chips):
    return pl.pallas_call(
        spread_body,
        out_shape=jax.ShapeDtypeStruct(
            (chips, coordinates.size // LANES, LANES), jnp.float32
        ),
        in_specs=[pl.BlockSpec(memory_space=pltpu.VMEM)],
        out_specs=pl.BlockSpec(memory_space=pltpu.VMEM),
        compiler_params=pltpu.CompilerParams(vmem_limit_bytes=SMALL_LIMIT),
        name="spread",
    )(coordinates)


def pick_body(groups, slots, places, own, twin, *outs):
    for d in range(1, groups):
        for i in range(2 * slots):
            side, w = i % 2, (groups - d) * slots + i // 2
            chip = lax.div(places[side, w], groups)
            outs[d - 1][i] = jnp.where(places[4 + side, w] > 0, twin[chip], own[chip])


def pick(places, own, twin, groups, slots):
    return pl.pallas_call(
        functools.partial(pick_body, groups, slots),
        out_shape=[jax.ShapeDtypeStruct((2 * slots, *own.shape[1:]), jnp.float32)] * (groups - 1),
        in_specs=[pl.BlockSpec(memory_space=pltpu.SMEM)]
        + [pl.BlockSpec(memory_space=pltpu.VMEM)] * 2,
        out_specs=[pl.BlockSpec(memory_space=pltpu.VMEM)] * (groups - 1),
        compiler_params=pltpu.CompilerParams(vmem_limit_bytes=SMALL_LIMIT),
        name="pick",
    )(places, own, twin)


def split3(x):
    high = x.astype(jnp.bfloat16).astype(jnp.float32)
    rest = x - high
    middle = rest.astype(jnp.bfloat16).astype(jnp.float32)
    low = (rest - middle).astype(jnp.bfloat16).astype(jnp.float32)
    return high, middle, low


def tile_body(rows, width, sc, delta_hbm, first, *refs):
    mine_here, twin_here, *others = refs[:-7]
    parts, delta, near, far, left, right, delta_sem = refs[-7:]
    slots = delta.shape[0]
    chunks = width // LANES
    f32, bf16 = jnp.float32, jnp.bfloat16

    def delta_copy(k):
        return pltpu.make_async_copy(delta_hbm.at[k], delta.at[k], delta_sem.at[k])

    @pl.when(sc[6, 0] > 0)
    def _():
        pltpu.make_async_copy(first, delta.at[0], delta_sem.at[0]).start()


    parts[2 * slots * DIM * chunks :, :] = jnp.zeros((8, LANES), f32)
    for ref in (near, far, left, right):
        ref[...] = jnp.zeros(ref.shape, f32)

    def one_tile(k, _):
        @pl.when(sc[6, k] > 0)
        def _():
            delta_copy(k).wait()
            later = jnp.minimum(k + 1, slots - 1)
            pl.when((k + 1 < slots) & (sc[6, later] > 0))(lambda: delta_copy(later).start())

            def block(side):
                groups = len(others) + 1
                chip, step = lax.div(sc[side, k], groups), lax.rem(sc[side, k], groups)
                found = jnp.where(sc[4 + side, k] > 0, twin_here[chip], mine_here[chip])
                for n, other in enumerate(others):
                    found = jnp.where(step == n + 1, other[2 * k + side], found)
                return [found[c * chunks : (c + 1) * chunks, :] for c in range(DIM)]

            xa, xb = block(0), block(1)
            mean = [jnp.sum(a, keepdims=True) * (1.0 / width) for a in xa]
            xa = [a - m for a, m in zip(xa, mean)]
            xb = [b - m for b, m in zip(xb, mean)]
            one = jnp.ones((chunks, LANES), f32)

            def terms(x):
                pieces = [split3(v) for v in x]
                norms = split3(x[0] * x[0] + x[1] * x[1] + x[2] * x[2])
                return pieces, list(norms)

            (pa, na), (pb, nb) = terms(xa), terms(xb)
            pairs = [(s, t) for s in range(3) for t in range(3)]
            la = [p[s] * -2.0 for p in pa for s, _ in pairs] + na + [one] * 3
            lb = [p[t] for p in pb for _, t in pairs] + [one] * 3 + nb
            va = [v for p in pa for v in p] + [one]
            vb = [v for p in pb for v in p] + [one]
            for ref, values in ((left, la), (right, lb), (near, va), (far, vb)):
                for n, v in enumerate(values):
                    ref[n] = v
            count = rows // STEP
            pieces = width // DEPTH

            def wide(ref, g):
                each = DEPTH // LANES
                return jnp.concatenate(
                    [ref[:, g * each + e, :] for e in range(each)], axis=1
                ).astype(bf16)

            lhs = [jnp.transpose(left[:, n, :]).astype(bf16) for n in range(count)]
            mine = [near[:, n, :].astype(bf16) for n in range(count)]
            mine = [jnp.concatenate([m, m], axis=1) for m in mine]
            cols = [wide(right, g) for g in range(pieces)]
            weights = [wide(far, g) for g in range(pieces)]
            stress = jnp.zeros((16, LANES), f32)
            row, col = [None] * count, [None] * pieces

            def front(n, g):
                return lax.dot_general(
                    lhs[n], cols[g], (((1,), (0,)), ((), ())), preferred_element_type=f32
                )

            def back(n, g, squared, stress):
                lanes = slice(g * DEPTH, (g + 1) * DEPTH)
                target = delta[k, n * STEP : (n + 1) * STEP, lanes].astype(f32)
                squared = jnp.maximum(squared, FLOOR_SQUARED)
                inverse = lax.rsqrt(squared)
                error = target - squared * inverse
                error = error * error
                for a in range(0, STEP, 16):
                    for b in range(0, DEPTH, LANES):
                        stress = stress + error[a : a + 16, b : b + LANES]
                ratio = target * inverse
                high = ratio.astype(bf16)
                low = (ratio - high.astype(f32)).astype(bf16)
                return stress, jnp.concatenate([high, low], axis=0)

            def last(n, g, both):
                a = lax.dot_general(
                    mine[n], both, (((1,), (0,)), ((), ())), preferred_element_type=f32
                )
                col[g] = a if col[g] is None else col[g] + a
                a = lax.dot_general(
                    weights[g], both, (((1,), (1,)), ((), ())), preferred_element_type=f32
                )
                row[n] = a if row[n] is None else row[n] + a

            order = [(n, g) for n in range(count) for g in range(pieces)]
            ahead = [front(*order[t]) for t in range(AHEAD)]
            held = []
            for t, (n, g) in enumerate(order):
                if t + AHEAD < len(order):
                    ahead.append(front(*order[t + AHEAD]))
                if len(held) > LAG - 1:
                    last(*held.pop(0))
                stress, both = back(n, g, ahead.pop(0), stress)
                held.append((n, g, both))
            for h in held:
                last(*h)
            row = [r[:, :STEP] + r[:, STEP:] for r in row]
            col = [c[:, e * LANES : (e + 1) * LANES] for c in col for e in range(DEPTH // LANES)]
            for side, own, total in ((0, xa, row), (1, xb, col)):
                first_row = (2 * k + side) * DIM * chunks
                for c in range(DIM):
                    for j in range(chunks):
                        t = total[j]
                        cross = t[3 * c : 3 * c + 1] + t[3 * c + 1 : 3 * c + 2] + t[3 * c + 2 : 3 * c + 3]
                        value = own[c][j : j + 1] * t[9:10] - cross
                        parts[pl.ds(first_row + c * chunks + j, 1), :] = value
            parts[2 * slots * DIM * chunks :, :] += stress[:8] + stress[8:]

        return 0

    lax.fori_loop(0, slots, one_tile, 0)


def tile_parts(scalars, dissim, first, sources):
    slots, rows, width = dissim.shape
    block_rows = DIM * width // LANES
    return pl.pallas_call(
        functools.partial(tile_body, rows, width),
        out_shape=jax.ShapeDtypeStruct((2 * slots * block_rows + 8, LANES), jnp.float32),
    in_specs=[pl.BlockSpec(memory_space=pltpu.SMEM), pl.BlockSpec(memory_space=pltpu.HBM)]
        + [pl.BlockSpec(memory_space=pltpu.VMEM)] * (1 + len(sources)),
        out_specs=pl.BlockSpec(memory_space=pltpu.VMEM),
        scratch_shapes=[
            pltpu.VMEM((slots, rows, width), jnp.bfloat16),
            pltpu.VMEM((16, rows // LANES, LANES), jnp.float32),
            pltpu.VMEM((16, width // LANES, LANES), jnp.float32),
            pltpu.VMEM((KDIM, rows // LANES, LANES), jnp.float32),
            pltpu.VMEM((KDIM, width // LANES, LANES), jnp.float32),
            pltpu.SemaphoreType.DMA((slots,)),
        ],
        compiler_params=pltpu.CompilerParams(vmem_limit_bytes=VMEM_LIMIT),
        name="tile_parts",
    )(
        scalars,
        pltpu.with_memory_space_constraint(dissim, pltpu.HBM),
        pltpu.with_memory_space_constraint(first, pltpu.VMEM),
        *sources,
    )


def gather_body(count, block_rows, where, *refs):
    sources, out = refs[:-1], refs[-1]
    stress = sources[0][count * block_rows :, :]
    for s in range(1, len(sources)):
        stress = stress + sources[s][count * block_rows :, :]
    for chip in range(out.shape[0]):
        out[chip, :block_rows, :] = jnp.zeros((block_rows, LANES), jnp.float32)
        out[chip, block_rows:, :] = stress
    for s in range(len(sources)):
        for i in range(count):
            chip = where[2 + i % 2, s * (count // 2) + i // 2]

            @pl.when(chip >= 0)
            def _(s=s, i=i, chip=chip):
                out[chip, :block_rows, :] += sources[s][
                    i * block_rows : (i + 1) * block_rows, :
                ]


def by_chip(where, sources, chips, slots):
    rows = sources[0].shape[0] - 8
    count = 2 * slots
    block_rows = rows // count
    return pl.pallas_call(
        functools.partial(gather_body, count, block_rows),
        out_shape=jax.ShapeDtypeStruct((chips, block_rows + 8, LANES), jnp.float32),
        in_specs=[pl.BlockSpec(memory_space=pltpu.SMEM)]
        + [pl.BlockSpec(memory_space=pltpu.VMEM)] * len(sources),
        out_specs=pl.BlockSpec(memory_space=pltpu.VMEM),
        compiler_params=pltpu.CompilerParams(vmem_limit_bytes=SMALL_LIMIT),
        name="by_chip",
    )(where, *sources)


def total_body(width, pieces, out, stress):
    block_rows = pieces.shape[1] - 8
    chunks = width // LANES
    total = pieces[0]
    for i in range(1, pieces.shape[0]):
        total = total + pieces[i]
    for c in range(DIM):
        for j in range(chunks):
            r = c * chunks + j
            out[c : c + 1, j * LANES : (j + 1) * LANES] = total[r : r + 1, :] * (1.0 / width)
    stress[0, 0] = jnp.sum(total[block_rows:, :])


def total_of(pieces, width):
    return pl.pallas_call(
        functools.partial(total_body, width),
        out_shape=(
            jax.ShapeDtypeStruct((DIM, width), jnp.float32),
            jax.ShapeDtypeStruct((1, 1), jnp.float32),
        ),
        in_specs=[pl.BlockSpec(memory_space=pltpu.VMEM)],
        out_specs=(
            pl.BlockSpec(memory_space=pltpu.VMEM),
            pl.BlockSpec(memory_space=pltpu.SMEM),
        ),
        compiler_params=pltpu.CompilerParams(vmem_limit_bytes=SMALL_LIMIT),
        name="total",
    )(pieces)


def prepare_body(groups, devs, slots, tiles_hbm, holder_hbm, delta_hbm, out, first, *scratch):
    tiles, holder, sem = scratch
    sources = (tiles_hbm, holder_hbm, delta_hbm.at[0])
    copies = [
        pltpu.make_async_copy(source, target, sem.at[i])
        for i, (source, target) in enumerate(zip(sources, (tiles, holder, first)))
    ]
    for copy in copies:
        copy.start()
    for copy in copies[:2]:
        copy.wait()
    f32, i32 = jnp.float32, jnp.int32
    group, dev = lax.axis_index("grp"), lax.axis_index("dev")
    count, blocks = tiles.shape[1], holder.shape[1]
    bits = devs.bit_length() - 1

    def column(row):
        return jnp.transpose(jnp.broadcast_to(row, (LANES, count)))[:, :1]

    owner = column(tiles[2:3, :])
    same = owner == tiles[2:3, :]
    later = lax.broadcasted_iota(i32, (count, count), 0) > lax.broadcasted_iota(
        i32, (count, count), 1
    )
    rank = jnp.sum(jnp.where(same & later, 1.0, 0.0), axis=1, keepdims=True)
    code = owner.astype(f32) * slots + rank
    lane = lax.broadcasted_iota(i32, (1, LANES), 1)
    order = lane // slots
    line = ((group + order) & (groups - 1)) * devs + (dev ^ (order // groups))
    wanted = (line * slots + (lane & (slots - 1))).astype(f32)
    chosen = (code == wanted) & (lane < 2 * groups * slots)
    numbers = lax.broadcasted_iota(i32, (count, blocks), 1)
    places = holder[...].astype(f32) + 1.0
    rows = []
    for side in range(2):
        found = jnp.where(column(tiles[side : side + 1, :]) == numbers, places, 0.0)
        found = jnp.sum(found, axis=1, keepdims=True)
        rows.append(jnp.sum(jnp.where(chosen, found, 0.0), axis=0, keepdims=True))
    held = [r.astype(i32) - 1 for r in rows]
    at = [jnp.maximum(h, 0) for h in held]
    chip = [(a & (devs - 1)) >> 1 for a in at]
    from_group = [(a >> bits) - group & (groups - 1) for a in at]
    twin = [(a ^ dev) & 1 for a in at]
    for side in range(2):
        here = (held[side] >= 0) & (from_group[side] == 0) & (twin[side] == 0)
        out[side : side + 1, :] = chip[side] * groups + from_group[side]
        out[2 + side : 3 + side, :] = jnp.where(here, chip[side], -1)
        out[4 + side : 5 + side, :] = twin[side]
    out[6:7, :] = jnp.where(held[0] >= 0, 1, 0)
    out[7:8, :] = jnp.zeros((1, LANES), i32)
    copies[2].wait()


def prepare(tile_list, holder, dissim, groups, devs):
    arrays = [tile_list.T, holder.reshape(1, -1)]
    return pl.pallas_call(
        functools.partial(prepare_body, groups, devs, dissim.shape[0]),
        out_shape=(
            jax.ShapeDtypeStruct((8, LANES), jnp.int32),
            pltpu.VMEM(dissim.shape[1:], dissim.dtype),
        ),
        in_specs=[pl.BlockSpec(memory_space=pltpu.HBM)] * 3,
        out_specs=[pl.BlockSpec(memory_space=pltpu.VMEM)] * 2,
        scratch_shapes=[pltpu.VMEM(a.shape, a.dtype) for a in arrays]
        + [pltpu.SemaphoreType.DMA((3,))],
        compiler_params=pltpu.CompilerParams(vmem_limit_bytes=SMALL_LIMIT),
        name="prepare",
    )(*[pltpu.with_memory_space_constraint(a, pltpu.HBM) for a in arrays + [dissim]])


def on_device(tile_list, holder, coordinates, dissim):
    groups, devs = lax.axis_size("grp"), lax.axis_size("dev")
    chips = devs // 2
    width = coordinates.shape[1]
    slots = dissim.shape[0]
    block_rows = DIM * width // LANES
    plane = plane_groups(groups, devs)
    sent = spread(coordinates, chips)
    own = lax.all_to_all(sent, AXES, 0, 0, tiled=True, axis_index_groups=plane)
    own, dissim = lax.optimization_barrier((own, dissim))
    twin = to_twin(own, groups * devs)
    places, first = prepare(tile_list, holder, dissim, groups, devs)
    picked = pick(places, own, twin, groups, slots)
    others = [
        lax.ppermute(picked[d - 1], AXES, line_perm(groups, devs, d)) for d in range(1, groups)
    ]
    parts = tile_parts(places, dissim, first, [own, twin, *others])
    line = from_line(parts, groups, devs)
    line = line + [to_twin(a, groups * devs) for a in line]
    pieces = by_chip(places, line, chips, slots)
    pieces = lax.all_to_all(pieces, AXES, 0, 0, tiled=True, axis_index_groups=plane)
    guttman, stress = total_of(pieces, width)
    return guttman, stress[0, 0]


def solution(mesh):
    placed = (P(), P(), P(None, AXES), P(AXES, None, None))
    return jax.shard_map(
        on_device,
        mesh=mesh,
        in_specs=placed,
        out_specs=(P(None, AXES), P()),
        check_vma=False,
    )
```

```python
import functools

import jax
import jax.numpy as jnp
from jax import lax
from jax.experimental import pallas as pl
from jax.experimental.pallas import tpu as pltpu
from jax.sharding import PartitionSpec as P

AXES = ("grp", "dev")
FLOOR_SQUARED = 0.0625
LANES = 128
DIM = 3
VMEM_LIMIT = 24 * 1024 * 1024
SMALL_LIMIT = 8 * 1024 * 1024
KDIM = 48
STEP = 128
DEPTH = 256
AHEAD = 6
LAG = 2


def line_perm(groups, devs, shift):
    return [
        (((g + shift) % groups) * devs + d, g * devs + d)
        for g in range(groups)
        for d in range(devs)
    ]


def core_perm(devices):
    return [(i, i ^ 1) for i in range(devices)]


def plane_groups(groups, devs):
    return [
        [g * devs + 2 * chip + core for chip in range(devs // 2)]
        for g in range(groups)
        for core in range(2)
    ]


def to_twin(array, devices):
    return lax.ppermute(array, AXES, core_perm(devices))


def from_line(array, groups, devs):
    return [array] + [
        lax.ppermute(array, AXES, line_perm(groups, devs, d)) for d in range(1, groups)
    ]


def spread_body(coords, out):
    rows = [
        coords[c : c + 1, j * LANES : (j + 1) * LANES]
        for c in range(DIM)
        for j in range(coords.shape[1] // LANES)
    ]
    block = jnp.concatenate(rows, axis=0)
    for chip in range(out.shape[0]):
        out[chip] = block


def spread(coordinates, chips):
    return pl.pallas_call(
        spread_body,
        out_shape=jax.ShapeDtypeStruct(
            (chips, coordinates.size // LANES, LANES), jnp.float32
        ),
        in_specs=[pl.BlockSpec(memory_space=pltpu.VMEM)],
        out_specs=pl.BlockSpec(memory_space=pltpu.VMEM),
        compiler_params=pltpu.CompilerParams(vmem_limit_bytes=SMALL_LIMIT),
        name="spread",
    )(coordinates)


def pick_body(groups, slots, places, own, twin, *outs):
    for d in range(1, groups):
        for i in range(2 * slots):
            side, w = i % 2, (groups - d) * slots + i // 2
            chip = lax.div(places[side, w], groups)
            outs[d - 1][i] = jnp.where(places[4 + side, w] > 0, twin[chip], own[chip])


def pick(places, own, twin, groups, slots):
    return pl.pallas_call(
        functools.partial(pick_body, groups, slots),
        out_shape=[jax.ShapeDtypeStruct((2 * slots, *own.shape[1:]), jnp.float32)] * (groups - 1),
        in_specs=[pl.BlockSpec(memory_space=pltpu.SMEM)]
        + [pl.BlockSpec(memory_space=pltpu.VMEM)] * 2,
        out_specs=[pl.BlockSpec(memory_space=pltpu.VMEM)] * (groups - 1),
        compiler_params=pltpu.CompilerParams(vmem_limit_bytes=SMALL_LIMIT),
        name="pick",
    )(places, own, twin)


def split3(x):
    high = x.astype(jnp.bfloat16).astype(jnp.float32)
    rest = x - high
    middle = rest.astype(jnp.bfloat16).astype(jnp.float32)
    low = (rest - middle).astype(jnp.bfloat16).astype(jnp.float32)
    return high, middle, low


def tile_body(rows, width, sc, delta_hbm, first, *refs):
    mine_here, twin_here, *others = refs[:-7]
    parts, delta, near, far, left, right, delta_sem = refs[-7:]
    slots = delta.shape[0]
    chunks = width // LANES
    f32, bf16 = jnp.float32, jnp.bfloat16

    def delta_copy(k):
        source = first.at[k] if k < 2 else delta_hbm.at[k]
        return pltpu.make_async_copy(source, delta.at[k], delta_sem.at[k])

    def await_delta(k):
        pltpu.make_async_copy(delta_hbm.at[k], delta.at[k], delta_sem.at[k]).wait()

    def held(m):
        both = (sc[6, 2 * m] > 0) & (sc[6, 2 * m + 1] > 0)
        return both, (sc[6, 2 * m] > 0) & jnp.logical_not(both)

    for m in range(slots // 2):
        both, alone = held(m)
        pl.when(both | alone)(lambda m=m: delta_copy(2 * m).start())
        pl.when(both)(lambda m=m: delta_copy(2 * m + 1).start())

    parts[2 * slots * DIM * chunks :, :] = jnp.zeros((8, LANES), f32)
    for ref in (near, far, left, right):
        ref[...] = jnp.zeros(ref.shape, f32)

    def one_tile(k, left, right, near, far):
        def block(side):
            groups = len(others) + 1
            chip, step = lax.div(sc[side, k], groups), lax.rem(sc[side, k], groups)
            found = jnp.where(sc[4 + side, k] > 0, twin_here[chip], mine_here[chip])
            for n, other in enumerate(others):
                found = jnp.where(step == n + 1, other[2 * k + side], found)
            return [found[c * chunks : (c + 1) * chunks, :] for c in range(DIM)]

        xa, xb = block(0), block(1)
        mean = [jnp.sum(a, keepdims=True) * (1.0 / width) for a in xa]
        xa = [a - m for a, m in zip(xa, mean)]
        xb = [b - m for b, m in zip(xb, mean)]
        one = jnp.ones((chunks, LANES), f32)

        def terms(x):
            pieces = [split3(v) for v in x]
            norms = split3(x[0] * x[0] + x[1] * x[1] + x[2] * x[2])
            return pieces, list(norms)

        (pa, na), (pb, nb) = terms(xa), terms(xb)
        pairs = [(s, t) for s in range(3) for t in range(3)]
        la = [p[s] * -2.0 for p in pa for s, _ in pairs] + na + [one] * 3
        lb = [p[t] for p in pb for _, t in pairs] + [one] * 3 + nb
        va = [v for p in pa for v in p] + [one]
        vb = [v for p in pb for v in p] + [one]
        for ref, values in ((left, la), (right, lb), (near, va), (far, vb)):
            for n, v in enumerate(values):
                ref[n] = v
        count = rows // STEP
        pieces = width // DEPTH

        def wide(ref, g):
            each = DEPTH // LANES
            return jnp.concatenate(
                [ref[:, g * each + e, :] for e in range(each)], axis=1
            ).astype(bf16)

        lhs = [jnp.transpose(left[:, n, :]).astype(bf16) for n in range(count)]
        mine = [near[:, n, :].astype(bf16) for n in range(count)]
        mine = [jnp.concatenate([m, m], axis=1) for m in mine]
        cols = [wide(right, g) for g in range(pieces)]
        weights = [wide(far, g) for g in range(pieces)]
        stress = jnp.zeros((16, LANES), f32)
        row, col = [None] * count, [None] * pieces

        def front(n, g):
            return lax.dot_general(
                lhs[n], cols[g], (((1,), (0,)), ((), ())), preferred_element_type=f32
            )

        def back(n, g, squared, stress):
            lanes = slice(g * DEPTH, (g + 1) * DEPTH)
            target = delta[k, n * STEP : (n + 1) * STEP, lanes].astype(f32)
            squared = jnp.maximum(squared, FLOOR_SQUARED)
            inverse = lax.rsqrt(squared)
            error = target - squared * inverse
            error = error * error
            for a in range(0, STEP, 16):
                for b in range(0, DEPTH, LANES):
                    stress = stress + error[a : a + 16, b : b + LANES]
            ratio = target * inverse
            high = ratio.astype(bf16)
            low = (ratio - high.astype(f32)).astype(bf16)
            return stress, jnp.concatenate([high, low], axis=0)

        def last(n, g, both):
            a = lax.dot_general(
                mine[n], both, (((1,), (0,)), ((), ())), preferred_element_type=f32
            )
            col[g] = a if col[g] is None else col[g] + a
            a = lax.dot_general(
                weights[g], both, (((1,), (1,)), ((), ())), preferred_element_type=f32
            )
            row[n] = a if row[n] is None else row[n] + a

        order = [(n, g) for n in range(count) for g in range(pieces)]
        ahead = [front(*order[t]) for t in range(AHEAD)]
        held = []
        for t, (n, g) in enumerate(order):
            if t + AHEAD < len(order):
                ahead.append(front(*order[t + AHEAD]))
            if len(held) > LAG - 1:
                last(*held.pop(0))
            stress, both = back(n, g, ahead.pop(0), stress)
            held.append((n, g, both))
        for h in held:
            last(*h)
        row = [r[:, :STEP] + r[:, STEP:] for r in row]
        col = [c[:, e * LANES : (e + 1) * LANES] for c in col for e in range(DEPTH // LANES)]
        for side, own, total in ((0, xa, row), (1, xb, col)):
            first_row = (2 * k + side) * DIM * chunks
            for c in range(DIM):
                for j in range(chunks):
                    t = total[j]
                    cross = t[3 * c : 3 * c + 1] + t[3 * c + 1 : 3 * c + 2] + t[3 * c + 2 : 3 * c + 3]
                    value = own[c][j : j + 1] * t[9:10] - cross
                    parts[pl.ds(first_row + c * chunks + j, 1), :] = value
        parts[2 * slots * DIM * chunks :, :] += stress[:8] + stress[8:]

    def two_slots(m, _):
        both, alone = held(m)

        @pl.when(both)
        def _():
            for s in range(2):
                await_delta(2 * m + s)
            for s in range(2):
                one_tile(2 * m + s, left.at[s], right.at[s], near.at[s], far.at[s])

        @pl.when(alone)
        def _():
            await_delta(2 * m)
            one_tile(2 * m, left.at[0], right.at[0], near.at[0], far.at[0])

        return 0

    lax.fori_loop(0, slots // 2, two_slots, 0)


def tile_parts(scalars, dissim, first, sources):
    slots, rows, width = dissim.shape
    block_rows = DIM * width // LANES
    return pl.pallas_call(
        functools.partial(tile_body, rows, width),
        out_shape=jax.ShapeDtypeStruct((2 * slots * block_rows + 8, LANES), jnp.float32),
    in_specs=[pl.BlockSpec(memory_space=pltpu.SMEM), pl.BlockSpec(memory_space=pltpu.HBM)]
        + [pl.BlockSpec(memory_space=pltpu.VMEM)] * (1 + len(sources)),
        out_specs=pl.BlockSpec(memory_space=pltpu.VMEM),
        scratch_shapes=[
            pltpu.VMEM((slots, rows, width), jnp.bfloat16),
            pltpu.VMEM((2, 16, rows // LANES, LANES), jnp.float32),
            pltpu.VMEM((2, 16, width // LANES, LANES), jnp.float32),
            pltpu.VMEM((2, KDIM, rows // LANES, LANES), jnp.float32),
            pltpu.VMEM((2, KDIM, width // LANES, LANES), jnp.float32),
            pltpu.SemaphoreType.DMA((slots,)),
        ],
        compiler_params=pltpu.CompilerParams(vmem_limit_bytes=VMEM_LIMIT),
        name="tile_parts",
    )(
        scalars,
        pltpu.with_memory_space_constraint(dissim, pltpu.HBM),
        pltpu.with_memory_space_constraint(first, pltpu.VMEM),
        *sources,
    )


def gather_body(count, block_rows, where, *refs):
    sources, out = refs[:-1], refs[-1]
    stress = sources[0][count * block_rows :, :]
    for s in range(1, len(sources)):
        stress = stress + sources[s][count * block_rows :, :]
    for chip in range(out.shape[0]):
        out[chip, :block_rows, :] = jnp.zeros((block_rows, LANES), jnp.float32)
        out[chip, block_rows:, :] = stress
    for s in range(len(sources)):
        for i in range(count):
            chip = where[2 + i % 2, s * (count // 2) + i // 2]

            @pl.when(chip >= 0)
            def _(s=s, i=i, chip=chip):
                out[chip, :block_rows, :] += sources[s][
                    i * block_rows : (i + 1) * block_rows, :
                ]


def by_chip(where, sources, chips, slots):
    rows = sources[0].shape[0] - 8
    count = 2 * slots
    block_rows = rows // count
    return pl.pallas_call(
        functools.partial(gather_body, count, block_rows),
        out_shape=jax.ShapeDtypeStruct((chips, block_rows + 8, LANES), jnp.float32),
        in_specs=[pl.BlockSpec(memory_space=pltpu.SMEM)]
        + [pl.BlockSpec(memory_space=pltpu.VMEM)] * len(sources),
        out_specs=pl.BlockSpec(memory_space=pltpu.VMEM),
        compiler_params=pltpu.CompilerParams(vmem_limit_bytes=SMALL_LIMIT),
        name="by_chip",
    )(where, *sources)


def total_body(width, pieces, out, stress):
    block_rows = pieces.shape[1] - 8
    chunks = width // LANES
    total = pieces[0]
    for i in range(1, pieces.shape[0]):
        total = total + pieces[i]
    for c in range(DIM):
        for j in range(chunks):
            r = c * chunks + j
            out[c : c + 1, j * LANES : (j + 1) * LANES] = total[r : r + 1, :] * (1.0 / width)
    stress[0, 0] = jnp.sum(total[block_rows:, :])


def total_of(pieces, width):
    return pl.pallas_call(
        functools.partial(total_body, width),
        out_shape=(
            jax.ShapeDtypeStruct((DIM, width), jnp.float32),
            jax.ShapeDtypeStruct((1, 1), jnp.float32),
        ),
        in_specs=[pl.BlockSpec(memory_space=pltpu.VMEM)],
        out_specs=(
            pl.BlockSpec(memory_space=pltpu.VMEM),
            pl.BlockSpec(memory_space=pltpu.SMEM),
        ),
        compiler_params=pltpu.CompilerParams(vmem_limit_bytes=SMALL_LIMIT),
        name="total",
    )(pieces)


def tables_body(groups, devs, slots, tiles_hbm, holder_hbm, out, *scratch):
    tiles, holder, sem = scratch
    sources = (tiles_hbm, holder_hbm)
    copies = [
        pltpu.make_async_copy(source, target, sem.at[i])
        for i, (source, target) in enumerate(zip(sources, (tiles, holder)))
    ]
    for copy in copies:
        copy.start()
    for copy in copies:
        copy.wait()
    f32, i32 = jnp.float32, jnp.int32
    group, dev = lax.axis_index("grp"), lax.axis_index("dev")
    count, blocks = tiles.shape[1], holder.shape[1]
    bits = devs.bit_length() - 1

    def column(row):
        return jnp.transpose(jnp.broadcast_to(row, (LANES, count)))[:, :1]

    owner = column(tiles[2:3, :])
    same = owner == tiles[2:3, :]
    later = lax.broadcasted_iota(i32, (count, count), 0) > lax.broadcasted_iota(
        i32, (count, count), 1
    )
    rank = jnp.sum(jnp.where(same & later, 1.0, 0.0), axis=1, keepdims=True)
    code = owner.astype(f32) * slots + rank
    lane = lax.broadcasted_iota(i32, (1, LANES), 1)
    order = lane // slots
    line = ((group + order) & (groups - 1)) * devs + (dev ^ (order // groups))
    wanted = (line * slots + (lane & (slots - 1))).astype(f32)
    chosen = (code == wanted) & (lane < 2 * groups * slots)
    numbers = lax.broadcasted_iota(i32, (count, blocks), 1)
    places = holder[...].astype(f32) + 1.0
    rows = []
    for side in range(2):
        found = jnp.where(column(tiles[side : side + 1, :]) == numbers, places, 0.0)
        found = jnp.sum(found, axis=1, keepdims=True)
        rows.append(jnp.sum(jnp.where(chosen, found, 0.0), axis=0, keepdims=True))
    held = [r.astype(i32) - 1 for r in rows]
    at = [jnp.maximum(h, 0) for h in held]
    chip = [(a & (devs - 1)) >> 1 for a in at]
    from_group = [(a >> bits) - group & (groups - 1) for a in at]
    twin = [(a ^ dev) & 1 for a in at]
    for side in range(2):
        here = (held[side] >= 0) & (from_group[side] == 0) & (twin[side] == 0)
        out[side : side + 1, :] = chip[side] * groups + from_group[side]
        out[2 + side : 3 + side, :] = jnp.where(here, chip[side], -1)
        out[4 + side : 5 + side, :] = twin[side]
    out[6:7, :] = jnp.where(held[0] >= 0, 1, 0)
    out[7:8, :] = jnp.zeros((1, LANES), i32)


def tables(tile_list, holder, groups, devs, slots):
    arrays = [tile_list.T, holder.reshape(1, -1)]
    return pl.pallas_call(
        functools.partial(tables_body, groups, devs, slots),
        out_shape=jax.ShapeDtypeStruct((8, LANES), jnp.int32),
        in_specs=[pl.BlockSpec(memory_space=pltpu.HBM)] * 2,
        out_specs=pl.BlockSpec(memory_space=pltpu.VMEM),
        scratch_shapes=[pltpu.VMEM(a.shape, a.dtype) for a in arrays]
        + [pltpu.SemaphoreType.DMA((2,))],
        compiler_params=pltpu.CompilerParams(vmem_limit_bytes=SMALL_LIMIT),
        name="tables",
    )(*[pltpu.with_memory_space_constraint(a, pltpu.HBM) for a in arrays])


def fetch_body(source, out, sem):
    copy = pltpu.make_async_copy(source.at[:2], out, sem)
    copy.start()
    copy.wait()


def first_tiles(dissim):
    return pl.pallas_call(
        fetch_body,
        out_shape=pltpu.VMEM((2, *dissim.shape[1:]), dissim.dtype),
        in_specs=[pl.BlockSpec(memory_space=pltpu.HBM)],
        out_specs=pl.BlockSpec(memory_space=pltpu.VMEM),
        scratch_shapes=[pltpu.SemaphoreType.DMA],
        compiler_params=pltpu.CompilerParams(vmem_limit_bytes=SMALL_LIMIT),
        name="first_tiles",
    )(pltpu.with_memory_space_constraint(dissim, pltpu.HBM))


def on_device(tile_list, holder, coordinates, dissim):
    groups, devs = lax.axis_size("grp"), lax.axis_size("dev")
    chips = devs // 2
    width = coordinates.shape[1]
    slots = dissim.shape[0]
    block_rows = DIM * width // LANES
    plane = plane_groups(groups, devs)
    sent = spread(coordinates, chips)
    own = lax.all_to_all(sent, AXES, 0, 0, tiled=True, axis_index_groups=plane)
    own, tile_list, holder = lax.optimization_barrier((own, tile_list, holder))
    twin = to_twin(own, groups * devs)
    places = tables(tile_list, holder, groups, devs, slots)
    picked = pick(places, own, twin, groups, slots)
    *picked, dissim = lax.optimization_barrier((*picked, dissim))
    first = first_tiles(dissim)
    others = [
        lax.ppermute(picked[d - 1], AXES, line_perm(groups, devs, d)) for d in range(1, groups)
    ]
    parts = tile_parts(places, dissim, first, [own, twin, *others])
    line = from_line(parts, groups, devs)
    line = line + [to_twin(a, groups * devs) for a in line]
    pieces = by_chip(places, line, chips, slots)
    pieces = lax.all_to_all(pieces, AXES, 0, 0, tiled=True, axis_index_groups=plane)
    guttman, stress = total_of(pieces, width)
    return guttman, stress[0, 0]


def solution(mesh):
    placed = (P(), P(), P(None, AXES), P(AXES, None, None))
    return jax.shard_map(
        on_device,
        mesh=mesh,
        in_specs=placed,
        out_specs=(P(None, AXES), P()),
        check_vma=False,
    )
```
